512 devices in a mesh: replica: 16 (over z_hi, y), fsdp: 32 (over x, z_lo, core).
Axes of the slice: x: 4, y: 4, z: 16 (z_hi: 4, z_lo: 4; z = z_hi * 4 + z_lo), core: 2. Of those that a mesh axis runs over, the one named last changes fastest.
Arguments:
- activations: bfloat16 [16, 8192, 4096], P('replica', 'fsdp'), may hold values from -6 to 6
- cotangent: bfloat16 [16, 8192, 512], P('replica', 'fsdp'), may hold values from -6 to 6
- local_weight: float32 [16, 3, 4096, 512], P('replica', None, 'fsdp'), may hold values from -6 to 6
- outer_weight: float32 [3, 4096, 512], P(None, 'fsdp'), may hold values from -6 to 6
- outer_moment: float32 [3, 4096, 512], P(None, 'fsdp'), may hold values from -3 to 3
- fragment_index: int32 [1], replicated, may hold values from 0 to 2
Outputs:
- keys: bfloat16 [16, 8192, 512], P('replica', 'fsdp')
- local_new: float32 [16, 3, 4096, 512], P('replica', None, 'fsdp')
- outer_new: float32 [4096, 512], P('fsdp')
- moment_new: float32 [4096, 512], P('fsdp')
The draws below stay inside these ranges and needn't reach their ends.
All inputs are finite; a program needn't handle non-finite values.
Results may differ from the reference program's by a relative error of at most 0.0085.
Values may be sent and summed in bfloat16 or wider, within the bound.
No kernel may reach another device: no remote copies, remote signals or barrier semaphores. Data moves between devices by JAX's collectives and lax.ppermute only.
A program may use at most 64 MiB of HBM per device.

```python
import jax
import jax.numpy as jnp
from jax import lax

DIN = 4096
KW = 512
TOK_DEV = 256
FRAGS = 3
REPLICAS = 16
TOK_REP = 8192
N_REPLICA = 16
N_FSDP = 32


def raised(array, own_key, source, target, blocks, factor):
    owner, partner = [(jnp.arange(array.shape[dim]) // (array.shape[dim] // blocks)).reshape([-1 if axis == dim else 1 for axis in range(array.ndim)]) for dim in (source, target)]
    chosen = jax.random.permutation(own_key, blocks)[partner]
    strong = (owner == chosen) | (owner == (partner + blocks // 2) % blocks)
    return jnp.where(strong, factor * array, array)


def levels(stream_key, dims, pieces, least, top_value):
    loudness = 1.0
    for position, shards_of in pieces:
        steps = jax.random.uniform(jax.random.fold_in(jax.random.fold_in(stream_key, 6), position), (shards_of,), jnp.float32, least / len(pieces), top_value / len(pieces))
        loudness = loudness * jnp.repeat(jnp.exp(steps), dims[position] // shards_of).reshape((-1,) + (1,) * (len(dims) - 1 - position))
    return loudness


def noise(key, dims, spread, reach, pieces=(), kind=jnp.bfloat16):
    drawn = jax.random.normal(key, dims, jnp.float32) * spread
    if len(pieces) > 0:
        drawn = levels(key, dims, pieces, -0.22, 0.18) * drawn
    return jnp.clip(drawn, min=-reach, max=reach).astype(kind)


def heavy_noise(rng, shape, scale, limit, split, heavy, dtype=jnp.bfloat16):
    array = scale * jax.random.normal(rng, shape, jnp.float32)
    if split:
        array = array * levels(rng, shape, split, -0.22, 0.18)
    return jnp.clip(raised(array, jax.random.fold_in(rng, 3), *heavy), -limit, limit).astype(dtype)


def setup_inputs(seed: int = 0) -> dict:
    arg_keys = jax.random.split(jax.random.key(seed), 7)
    return {
        "activations": heavy_noise(arg_keys[0], (REPLICAS, TOK_REP, DIN), 1.0, 6.0, ((0, 16), (1, 32)), (1, 2, 32, 2.75)),
        "cotangent": noise(arg_keys[1], (REPLICAS, TOK_REP, KW), 1.0, 6.0, ((0, 16), (1, 32))),
        "local_weight": noise(arg_keys[2], (REPLICAS, FRAGS, DIN, KW), 1.0, 6.0, ((0, 16), (2, 32)), jnp.float32),
        "outer_weight": noise(arg_keys[3], (FRAGS, DIN, KW), 1.0, 6.0, ((1, 32),), jnp.float32),
        "outer_moment": noise(arg_keys[4], (FRAGS, DIN, KW), 0.5, 3.0, ((1, 32),), jnp.float32),
        "fragment_index": jax.random.randint(arg_keys[5], (1,), 0, FRAGS).astype(jnp.int32),
    }


inner_rate = 0.25
outer_rate = 0.7
momentum_factor = 0.9
mixing = 0.5


def reference(activations, cotangent, local_weight, outer_weight, outer_moment, fragment_index):
    scale = DIN ** -0.5
    chosen = fragment_index[0]

    def replica_step(packed):
        inputs, upstream, layers = packed
        weights = layers[0].astype(jnp.bfloat16)
        keys = (jnp.dot(inputs, weights, preferred_element_type=jnp.float32) * scale).astype(jnp.bfloat16)
        input_blocks = inputs.reshape(N_FSDP, TOK_DEV, DIN)
        upstream_blocks = upstream.reshape(N_FSDP, TOK_DEV, KW)

        def add_part(total, pair):
            block_in, block_up = pair
            part = jnp.dot(block_in.T, block_up, preferred_element_type=jnp.float32) * scale
            part = lax.optimization_barrier(part.astype(jnp.bfloat16))
            return total + part.astype(jnp.float32), None

        gradient, unused = lax.scan(add_part, jnp.zeros((DIN, KW), jnp.float32), (input_blocks, upstream_blocks))
        updated = layers.at[0].set(layers[0] - inner_rate * gradient)
        return keys, updated

    keys, updated = lax.map(replica_step, (activations, cotangent, local_weight))
    selected = lax.dynamic_index_in_dim(updated, chosen, 1, keepdims=False)
    old_outer = lax.dynamic_index_in_dim(outer_weight, chosen, 0, keepdims=False)
    old_moment = lax.dynamic_index_in_dim(outer_moment, chosen, 0, keepdims=False)
    delta = old_outer[None] - selected
    average = jnp.sum(delta, axis=0) / N_REPLICA
    moment_new = momentum_factor * old_moment + average
    outer_new = old_outer - outer_rate * (average + momentum_factor * moment_new)
    mixed = mixing * selected + (1.0 - mixing) * outer_new[None]
    chosen_mask = (jnp.arange(FRAGS) == chosen)[None, :, None, None]
    local_new = jnp.where(chosen_mask, mixed[:, None], updated)
    return keys, local_new, outer_new, moment_new
```

```python
import jax
import jax.numpy as jnp
from jax import lax
from jax.experimental import pallas as pl
from jax.experimental.pallas import tpu as pltpu
from jax.sharding import Mesh, PartitionSpec as P

inner_rate = 0.25
outer_rate = 0.7
momentum_factor = 0.9
mixing = 0.5

SIDE = 4
CORES = 2
PIECE = 128


def pick_kernel(core_ref, all_ref, picked_ref, sems):
    runs = picked_ref.shape[1] // PIECE
    copies = []
    for run in range(runs):
        start = pl.multiple_of((2 * run + core_ref[0]) * PIECE, PIECE)
        copies.append(
            pltpu.make_async_copy(
                all_ref.at[:, pl.ds(start, PIECE)],
                picked_ref.at[:, pl.ds(run * PIECE, PIECE)],
                sems.at[run],
            )
        )
    for copy in copies:
        copy.start()
    for copy in copies:
        copy.wait()


def pick(inputs, core):
    tokens, width = inputs.shape
    return pl.pallas_call(
        pick_kernel,
        out_shape=jax.ShapeDtypeStruct((tokens, width // CORES), inputs.dtype),
        in_specs=[
            pl.BlockSpec(memory_space=pltpu.SMEM),
            pl.BlockSpec(memory_space=pl.ANY),
        ],
        out_specs=pl.BlockSpec(memory_space=pl.ANY),
        scratch_shapes=[pltpu.SemaphoreType.DMA((width // CORES // PIECE,))],
        name="pick_columns",
    )(core, inputs)


def grad_kernel(core_ref, mine_ref, theirs_ref, up_ref, their_up_ref, out_ref):
    scale = 4096 ** (-0.5)
    dims = (((0,), (0,)), ((), ()))
    for run in range(SIDE):
        start = pl.multiple_of((2 * run + core_ref[0]) * PIECE, PIECE)
        total = lax.dot_general(
            mine_ref[:, pl.ds(start, PIECE)], up_ref[...], dims, preferred_element_type=jnp.float32
        )
        total += lax.dot_general(
            theirs_ref[:, run * PIECE : (run + 1) * PIECE],
            their_up_ref[...],
            dims,
            preferred_element_type=jnp.float32,
        )
        out_ref[0, run * PIECE : (run + 1) * PIECE, :] = (total * scale).astype(out_ref.dtype)


def grad(core, mine, theirs, up, their_up):
    tokens, width = mine.shape
    features = up.shape[1]
    rows = SIDE * PIECE
    whole = lambda i, core_ref: (0, 0)
    return pl.pallas_call(
        grad_kernel,
        out_shape=jax.ShapeDtypeStruct((SIDE, rows, features), jnp.bfloat16),
        grid_spec=pltpu.PrefetchScalarGridSpec(
            num_scalar_prefetch=1,
            grid=(SIDE,),
            in_specs=[
                pl.BlockSpec((tokens, CORES * rows), lambda i, core_ref: (0, i)),
                pl.BlockSpec((tokens, rows), lambda i, core_ref: (0, i)),
                pl.BlockSpec((tokens, features), whole),
                pl.BlockSpec((tokens, features), whole),
            ],
            out_specs=pl.BlockSpec((1, rows, features), lambda i, core_ref: (i, 0, 0)),
        ),
        name="gradient",
    )(core, mine, theirs, up, their_up)


def shards(activations, cotangent, local_weight, outer_weight, outer_moment, fragment_index):
    inputs = activations[0]
    upstream = cotangent[0]
    layers = local_weight[0]
    scale = inputs.shape[1] ** (-0.5)
    trained = layers[0].astype(jnp.bfloat16)
    chosen = fragment_index[0]
    replicas = lax.axis_size("zh") * lax.axis_size("y")
    features = upstream.shape[1]
    core = lax.axis_index("c").astype(jnp.int32)

    gathered = lax.all_gather(trained, ("x", "zl", "c"), axis=0, tiled=True)

    swap = [(0, 1), (1, 0)]
    their_up = lax.ppermute(upstream, "c", swap)
    theirs = lax.ppermute(pick(inputs, (1 - core)[None]), "c", swap)
    part = grad(core[None], inputs, theirs, upstream, their_up)

    part = lax.all_to_all(part, "x", 0, 0)
    part = jnp.sum(part.astype(jnp.float32), axis=0).astype(jnp.bfloat16)
    part = lax.all_to_all(part.reshape(SIDE, PIECE, features), "zl", 0, 0)
    gradient = jnp.sum(part.astype(jnp.float32), axis=0)

    old_outer = lax.dynamic_index_in_dim(outer_weight, chosen, 0, keepdims=False)
    old_moment = lax.dynamic_index_in_dim(outer_moment, chosen, 0, keepdims=False)
    stale = lax.dynamic_index_in_dim(layers, chosen, 0, keepdims=False)
    selected = stale - inner_rate * jnp.where(chosen == 0, gradient, 0.0)
    delta = (old_outer - selected).astype(jnp.bfloat16)
    quarter = PIECE // SIDE
    total = lax.all_to_all(delta.reshape(SIDE, quarter, features), "y", 0, 0)
    total = jnp.sum(total.astype(jnp.float32), axis=0).astype(jnp.bfloat16)
    total = jnp.broadcast_to(total[None], (SIDE, quarter, features))
    total = lax.all_to_all(total, "zh", 0, 0)
    average = (jnp.sum(total.astype(jnp.float32), axis=0) / replicas).astype(jnp.bfloat16)
    average = jnp.broadcast_to(average[None], (SIDE, quarter, features))
    average = lax.all_to_all(average, "y", 0, 0).reshape(PIECE, features).astype(jnp.float32)

    summed = jnp.dot(inputs, gathered, preferred_element_type=jnp.float32)
    keys = (summed * scale).astype(jnp.bfloat16)[None]

    moment_new = momentum_factor * old_moment + average
    outer_new = old_outer - outer_rate * (average + momentum_factor * moment_new)
    mixed = mixing * selected + (1.0 - mixing) * outer_new
    number = jnp.arange(layers.shape[0])[:, None, None]
    updated = jnp.where(number == 0, layers - inner_rate * gradient[None], layers)
    local_new = jnp.where(number == chosen, mixed[None], updated)[None]
    return (keys, local_new, outer_new, moment_new)


def solution(mesh):
    fine = Mesh(
        mesh.devices.reshape(SIDE, SIDE, SIDE, SIDE, CORES), ("zh", "y", "x", "zl", "c")
    )
    replica = ("zh", "y")
    fsdp = ("x", "zl", "c")
    in_specs = (
        P(replica, fsdp, None),
        P(replica, fsdp, None),
        P(replica, None, fsdp, None),
        P(None, fsdp, None),
        P(None, fsdp, None),
        P(),
    )
    out_specs = (
        P(replica, fsdp, None),
        P(replica, None, fsdp, None),
        P(fsdp, None),
        P(fsdp, None),
    )
    return jax.shard_map(shards, mesh=fine, in_specs=in_specs, out_specs=out_specs, check_vma=False)
```

```python
import jax
import jax.numpy as jnp
from jax import lax
from jax.experimental import pallas as pl
from jax.experimental.pallas import tpu as pltpu
from jax.sharding import Mesh, PartitionSpec as P

inner_rate = 0.25
outer_rate = 0.7
momentum_factor = 0.9
mixing = 0.5

SIDE = 4
CORES = 2
PIECE = 128
ROWS = SIDE * PIECE
QUARTER = PIECE // SIDE
SCALE = 4096 ** (-0.5)

VMEM_LIMIT = 56 << 20

bf16 = jnp.bfloat16
f32 = jnp.float32


def core_columns(ref, core, chunk=0):
    runs = []
    for run in range(SIDE):
        start = ((chunk * SIDE + run) * CORES + core) * PIECE
        runs.append(ref[:, pl.ds(pl.multiple_of(start, PIECE), PIECE)])
    return jnp.concatenate(runs, axis=1)


def grad_kernel(place_ref, inputs_ref, theirs_ref, up_ref, their_up_ref, out_ref):
    dims = (((0,), (0,)), ((), ()))
    core = place_ref[1]
    total = lax.dot_general(
        core_columns(inputs_ref, core), up_ref[...], dims, preferred_element_type=f32
    )
    total += lax.dot_general(
        core_columns(theirs_ref, core), their_up_ref[...], dims, preferred_element_type=f32
    )
    out_ref[0] = (total * SCALE).astype(bf16)


def grad(place, inputs, theirs, up, their_up):
    tokens = inputs.shape[0]
    features = up.shape[1]
    wide = pl.BlockSpec((tokens, CORES * ROWS), lambda i, place: (0, i))
    whole = pl.BlockSpec((tokens, features), lambda i, place: (0, 0))
    return pl.pallas_call(
        grad_kernel,
        out_shape=jax.ShapeDtypeStruct((SIDE, ROWS, features), bf16),
        grid_spec=pltpu.PrefetchScalarGridSpec(
            num_scalar_prefetch=1,
            grid=(SIDE,),
            in_specs=[wide, wide, whole, whole],
            out_specs=pl.BlockSpec((1, ROWS, features), lambda i, place: (i, 0, 0)),
        ),
        cost_estimate=pl.CostEstimate(flops=1 << 30, bytes_accessed=6 << 20, transcendentals=0),
        compiler_params=pltpu.CompilerParams(vmem_limit_bytes=VMEM_LIMIT),
        name="gradient",
    )(place, inputs, theirs, up, their_up)


def cast_kernel(after_ref, layer_ref, out_ref):
    out_ref[...] = layer_ref[0].astype(bf16)


def cast(layers, after):
    features = layers.shape[2]
    return pl.pallas_call(
        cast_kernel,
        out_shape=jax.ShapeDtypeStruct((PIECE, features), bf16),
        grid=(1,),
        in_specs=[
            pl.BlockSpec(memory_space=pl.ANY),
            pl.BlockSpec((1, PIECE, features), lambda i: (0, 0, 0)),
        ],
        out_specs=pl.BlockSpec((PIECE, features), lambda i: (0, 0)),
        cost_estimate=pl.CostEstimate(flops=0, bytes_accessed=1 << 20, transcendentals=0),
        name="cast_weights",
    )(after, layers)


def their_keys_kernel(place_ref, theirs_ref, *refs):
    total = 0.0
    for offset in range(SIDE):
        chunk = lax.rem(place_ref[0] + SIDE - offset, SIDE)
        columns = core_columns(theirs_ref, place_ref[1], chunk)
        total += jnp.dot(columns, refs[offset][...], preferred_element_type=f32)
    refs[-1][...] = (total * SCALE).astype(bf16)


def their_keys(place, theirs, weights):
    tokens = theirs.shape[0]
    features = weights[0].shape[1]
    return pl.pallas_call(
        their_keys_kernel,
        out_shape=jax.ShapeDtypeStruct((tokens, features), bf16),
        in_specs=[pl.BlockSpec(memory_space=pltpu.SMEM)]
        + [pl.BlockSpec(memory_space=pltpu.VMEM)] * (1 + SIDE),
        out_specs=pl.BlockSpec(memory_space=pltpu.VMEM),
        cost_estimate=pl.CostEstimate(flops=1 << 29, bytes_accessed=3 << 20, transcendentals=0),
        compiler_params=pltpu.CompilerParams(vmem_limit_bytes=VMEM_LIMIT),
        name="their_keys",
    )(place, theirs, *weights)


def own_keys_kernel(place_ref, inputs_ref, other_ref, *refs):
    total = 0.0
    for offset in range(SIDE):
        chunk = lax.rem(place_ref[0] + SIDE - offset, SIDE)
        columns = core_columns(inputs_ref, place_ref[1], chunk)
        total += jnp.dot(columns, refs[offset][...], preferred_element_type=f32)
    refs[-1][0] = (total * SCALE + other_ref[...].astype(f32)).astype(bf16)


def own_keys(place, inputs, weights, other):
    tokens = inputs.shape[0]
    features = weights[0].shape[1]
    return pl.pallas_call(
        own_keys_kernel,
        out_shape=jax.ShapeDtypeStruct((1, tokens, features), bf16),
        in_specs=[pl.BlockSpec(memory_space=pltpu.SMEM)]
        + [pl.BlockSpec(memory_space=pltpu.VMEM)] * (2 + SIDE),
        out_specs=pl.BlockSpec(memory_space=pltpu.VMEM),
        cost_estimate=pl.CostEstimate(flops=1 << 29, bytes_accessed=4 << 20, transcendentals=0),
        compiler_params=pltpu.CompilerParams(vmem_limit_bytes=VMEM_LIMIT),
        name="own_keys",
    )(place, inputs, other, *weights)


def update_kernel(parts_ref, layers_ref, out_ref):
    gradient = parts_ref[0].astype(f32)
    for other in range(1, parts_ref.shape[0]):
        gradient += parts_ref[other].astype(f32)
    out_ref[0, 0] = layers_ref[0, 0] - inner_rate * gradient


def update(parts, layers):
    rows, features = layers.shape[2:]
    steps = 2
    block = rows // steps
    layer = pl.BlockSpec((1, 1, block, features), lambda i: (0, 0, i, 0))
    return pl.pallas_call(
        update_kernel,
        out_shape=jax.ShapeDtypeStruct(layers.shape, f32),
        grid=(steps,),
        in_specs=[pl.BlockSpec((parts.shape[0], block, features), lambda i: (0, i, 0)), layer],
        out_specs=layer,
        input_output_aliases={1: 0},
        cost_estimate=pl.CostEstimate(flops=1 << 19, bytes_accessed=1 << 20, transcendentals=0),
        compiler_params=pltpu.CompilerParams(vmem_limit_bytes=VMEM_LIMIT),
        name="update",
    )(parts, layers)


def settle_kernel(
    chosen_ref, average_ref, layer_ref, outer_ref, moment_ref, layer_out, outer_out, moment_out
):
    average = average_ref[...].astype(f32)
    moment = momentum_factor * moment_ref[0] + average
    outer = outer_ref[0] - outer_rate * (average + momentum_factor * moment)
    moment_out[...] = moment
    outer_out[...] = outer
    layer_out[0, 0] = mixing * layer_ref[0, 0] + (1.0 - mixing) * outer


def settle(chosen, average, updated, outer_weight, outer_moment):
    rows, features = updated.shape[2:]
    steps = 2
    block = rows // steps
    picked = pl.BlockSpec((1, block, features), lambda i, chosen: (chosen[0], i, 0))
    layer = pl.BlockSpec((1, 1, block, features), lambda i, chosen: (0, chosen[0], i, 0))
    flat = pl.BlockSpec((block, features), lambda i, chosen: (i, 0))
    return pl.pallas_call(
        settle_kernel,
        out_shape=(
            jax.ShapeDtypeStruct(updated.shape, f32),
            jax.ShapeDtypeStruct((rows, features), f32),
            jax.ShapeDtypeStruct((rows, features), f32),
        ),
        grid_spec=pltpu.PrefetchScalarGridSpec(
            num_scalar_prefetch=1,
            grid=(steps,),
            in_specs=[flat, layer, picked, picked],
            out_specs=(layer, flat, flat),
        ),
        input_output_aliases={2: 0},
        cost_estimate=pl.CostEstimate(flops=1 << 20, bytes_accessed=2 << 20, transcendentals=0),
        compiler_params=pltpu.CompilerParams(vmem_limit_bytes=VMEM_LIMIT),
        name="settle",
    )(chosen, average, updated, outer_weight, outer_moment)


def sum_all(parts):
    terms = [parts[index].astype(f32) for index in range(parts.shape[0])]
    while len(terms) > 1:
        terms = [first + second for first, second in zip(terms[::2], terms[1::2])]
    return terms[0]


def spread(rows):
    return jnp.broadcast_to(rows.astype(bf16)[None], (SIDE,) + rows.shape)


def shift(offset):
    return [(source, (source + offset) % SIDE) for source in range(SIDE)]


swap = [(0, 1), (1, 0)]


def shards(activations, cotangent, local_weight, outer_weight, outer_moment, fragment_index):
    inputs = activations[0]
    upstream = cotangent[0]
    layers = local_weight[0]
    features = upstream.shape[1]
    chosen = fragment_index[0]
    place = jnp.stack([lax.axis_index(name) for name in ("x", "c")]).astype(jnp.int32)

    theirs = lax.ppermute(inputs, "c", swap)
    their_up = lax.ppermute(upstream, "c", swap)
    part = grad(place, inputs, theirs, upstream, their_up)
    rows = lax.all_gather(cast(layers, part), "zl", axis=0, tiled=True)
    pick = lambda array: lax.dynamic_index_in_dim(array, chosen, 0, keepdims=False)
    delta = pick(outer_weight) - pick(layers)
    part = lax.all_to_all(part, "x", 0, 0)
    part, rows, delta = lax.optimization_barrier((part, rows, delta))

    part = sum_all(part).astype(bf16).reshape(SIDE, PIECE, features)
    part = lax.all_to_all(part, "zl", 0, 0)
    weights = [rows] + [lax.ppermute(rows, "x", shift(offset)) for offset in (1, 2, 3)]

    mean = delta + jnp.where(chosen == 0, inner_rate, 0.0) * sum_all(part)
    mean = mean.astype(bf16).reshape(SIDE, QUARTER, features)
    mean = sum_all(lax.all_to_all(mean, "y", 0, 0)) * (1.0 / (SIDE * SIDE))
    mean, weights[1], weights[3] = lax.optimization_barrier((mean, weights[1], weights[3]))
    mean = sum_all(lax.all_to_all(spread(mean), "zh", 0, 0))
    mean = lax.all_to_all(spread(mean), "y", 0, 0).reshape(PIECE, features)

    updated = update(part, local_weight)
    other = lax.ppermute(their_keys(place, theirs, weights), "c", swap)
    keys = own_keys(place, inputs, weights, other)
    local_new, outer_new, moment_new = settle(
        fragment_index, mean, updated, outer_weight, outer_moment
    )
    return keys, local_new, outer_new, moment_new


def solution(mesh):
    fine = Mesh(
        mesh.devices.reshape(SIDE, SIDE, SIDE, SIDE, CORES), ("zh", "y", "x", "zl", "c")
    )
    replica = ("zh", "y")
    fsdp = ("x", "zl", "c")
    in_specs = (
        P(replica, fsdp, None),
        P(replica, fsdp, None),
        P(replica, None, fsdp, None),
        P(None, fsdp, None),
        P(None, fsdp, None),
        P(),
    )
    out_specs = (
        P(replica, fsdp, None),
        P(replica, None, fsdp, None),
        P(fsdp, None),
        P(fsdp, None),
    )
    return jax.shard_map(shards, mesh=fine, in_specs=in_specs, out_specs=out_specs, check_vma=False)
```

```python
import jax
import jax.numpy as jnp
from jax import lax
from jax.experimental import pallas as pl
from jax.experimental.pallas import tpu as pltpu
from jax.sharding import Mesh, PartitionSpec as P

inner_rate = 0.25
outer_rate = 0.7
momentum_factor = 0.9
mixing = 0.5

SIDE = 4
CORES = 2
PIECE = 128
ROWS = SIDE * PIECE
QUARTER = PIECE // SIDE
SCALE = 4096 ** (-0.5)

VMEM_LIMIT = 56 << 20
GRAD_VMEM_LIMIT = 60 << 20

bf16 = jnp.bfloat16
f32 = jnp.float32


def core_columns(ref, core, chunk=0):
    runs = []
    for run in range(SIDE):
        start = ((chunk * SIDE + run) * CORES + core) * PIECE
        runs.append(ref[:, pl.ds(pl.multiple_of(start, PIECE), PIECE)])
    return jnp.concatenate(runs, axis=1)


def grad_kernel(
    place_ref, inputs_hbm, theirs_hbm, up_hbm, their_up_hbm, out_hbm, inputs, ups, out, in_sems, out_sems
):
    tokens = inputs_hbm.shape[0]
    copies = [
        pltpu.make_async_copy(inputs_hbm, inputs.at[:tokens], in_sems.at[0]),
        pltpu.make_async_copy(theirs_hbm, inputs.at[tokens:], in_sems.at[1]),
        pltpu.make_async_copy(up_hbm, ups.at[:tokens], in_sems.at[2]),
        pltpu.make_async_copy(their_up_hbm, ups.at[tokens:], in_sems.at[3]),
    ]
    for copy in copies:
        copy.start()
    for copy in copies:
        copy.wait()
    stores = []
    for chunk in range(SIDE):
        total = lax.dot_general(
            core_columns(inputs, place_ref[1], chunk),
            ups[...],
            (((0,), (0,)), ((), ())),
            preferred_element_type=f32,
        )
        out[chunk] = (total * SCALE).astype(bf16)
        stores.append(pltpu.make_async_copy(out.at[chunk], out_hbm.at[chunk], out_sems.at[chunk]))
        stores[-1].start()
    for store in stores:
        store.wait()


def grad(place, inputs, theirs, up, their_up):
    tokens, width = inputs.shape
    features = up.shape[1]
    anywhere = pl.BlockSpec(memory_space=pl.ANY)
    return pl.pallas_call(
        grad_kernel,
        out_shape=jax.ShapeDtypeStruct((SIDE, ROWS, features), bf16),
        in_specs=[pl.BlockSpec(memory_space=pltpu.SMEM)] + [anywhere] * 4,
        out_specs=anywhere,
        scratch_shapes=[
            pltpu.VMEM((2 * tokens, width), bf16),
            pltpu.VMEM((2 * tokens, features), bf16),
            pltpu.VMEM((SIDE, ROWS, features), bf16),
            pltpu.SemaphoreType.DMA((4,)),
            pltpu.SemaphoreType.DMA((SIDE,)),
        ],
        cost_estimate=pl.CostEstimate(flops=1 << 30, bytes_accessed=6 << 20, transcendentals=0),
        compiler_params=pltpu.CompilerParams(vmem_limit_bytes=GRAD_VMEM_LIMIT),
        name="gradient",
    )(place, inputs, theirs, up, their_up)


def cast_kernel(after_ref, layer_ref, out_ref):
    out_ref[...] = layer_ref[0].astype(bf16)


def cast(layers, after):
    features = layers.shape[2]
    return pl.pallas_call(
        cast_kernel,
        out_shape=jax.ShapeDtypeStruct((PIECE, features), bf16),
        grid=(1,),
        in_specs=[
            pl.BlockSpec(memory_space=pl.ANY),
            pl.BlockSpec((1, PIECE, features), lambda i: (0, 0, 0)),
        ],
        out_specs=pl.BlockSpec((PIECE, features), lambda i: (0, 0)),
        cost_estimate=pl.CostEstimate(flops=0, bytes_accessed=1 << 20, transcendentals=0),
        name="cast_weights",
    )(after, layers)


def their_keys_kernel(place_ref, after_ref, theirs_ref, *refs):
    total = 0.0
    for offset in range(SIDE):
        chunk = lax.rem(place_ref[0] + SIDE - offset, SIDE)
        columns = core_columns(theirs_ref, place_ref[1], chunk)
        total += jnp.dot(columns, refs[offset][...], preferred_element_type=f32)
    refs[-1][...] = (total * SCALE).astype(bf16)


def their_keys(place, theirs, weights, after):
    tokens = theirs.shape[0]
    features = weights[0].shape[1]
    return pl.pallas_call(
        their_keys_kernel,
        out_shape=jax.ShapeDtypeStruct((tokens, features), bf16),
        in_specs=[pl.BlockSpec(memory_space=pltpu.SMEM), pl.BlockSpec(memory_space=pl.ANY)]
        + [pl.BlockSpec(memory_space=pltpu.VMEM)] * (1 + SIDE),
        out_specs=pl.BlockSpec(memory_space=pltpu.VMEM),
        cost_estimate=pl.CostEstimate(flops=1 << 29, bytes_accessed=3 << 20, transcendentals=0),
        compiler_params=pltpu.CompilerParams(vmem_limit_bytes=VMEM_LIMIT),
        name="their_keys",
    )(place, after, theirs, *weights)


def own_keys_kernel(place_ref, inputs_ref, other_ref, *refs):
    total = 0.0
    for offset in range(SIDE):
        chunk = lax.rem(place_ref[0] + SIDE - offset, SIDE)
        columns = core_columns(inputs_ref, place_ref[1], chunk)
        total += jnp.dot(columns, refs[offset][...], preferred_element_type=f32)
    refs[-1][0] = (total * SCALE + other_ref[...].astype(f32)).astype(bf16)


def own_keys(place, inputs, weights, other):
    tokens = inputs.shape[0]
    features = weights[0].shape[1]
    return pl.pallas_call(
        own_keys_kernel,
        out_shape=jax.ShapeDtypeStruct((1, tokens, features), bf16),
        in_specs=[pl.BlockSpec(memory_space=pltpu.SMEM)]
        + [pl.BlockSpec(memory_space=pltpu.VMEM)] * (2 + SIDE),
        out_specs=pl.BlockSpec(memory_space=pltpu.VMEM),
        cost_estimate=pl.CostEstimate(flops=1 << 29, bytes_accessed=4 << 20, transcendentals=0),
        compiler_params=pltpu.CompilerParams(vmem_limit_bytes=VMEM_LIMIT),
        name="own_keys",
    )(place, inputs, other, *weights)


def update_kernel(parts_ref, layers_ref, out_ref):
    gradient = parts_ref[0].astype(f32)
    for other in range(1, SIDE):
        gradient += parts_ref[other].astype(f32)
    out_ref[0, 0] = layers_ref[0, 0] - inner_rate * gradient
    for layer in range(1, layers_ref.shape[1]):
        out_ref[0, layer] = layers_ref[0, layer]


def update(parts, local_weight):
    count, rows, features = local_weight.shape[1:]
    steps = 2
    block = rows // steps
    layers = pl.BlockSpec((1, count, block, features), lambda i: (0, 0, i, 0))
    return pl.pallas_call(
        update_kernel,
        out_shape=jax.ShapeDtypeStruct(local_weight.shape, f32),
        grid=(steps,),
        in_specs=[pl.BlockSpec((SIDE, block, features), lambda i: (0, i, 0)), layers],
        out_specs=layers,
        cost_estimate=pl.CostEstimate(flops=1 << 19, bytes_accessed=2 << 20, transcendentals=0),
        compiler_params=pltpu.CompilerParams(vmem_limit_bytes=VMEM_LIMIT),
        name="update",
    )(parts, local_weight)


def settle_kernel(
    chosen_ref, average_ref, layer_ref, outer_ref, moment_ref, layer_out, outer_out, moment_out
):
    average = average_ref[...].astype(f32)
    moment = momentum_factor * moment_ref[0] + average
    outer = outer_ref[0] - outer_rate * (average + momentum_factor * moment)
    moment_out[...] = moment
    outer_out[...] = outer
    layer_out[0, 0] = mixing * layer_ref[0, 0] + (1.0 - mixing) * outer


def settle(chosen, average, updated, outer_weight, outer_moment):
    rows, features = updated.shape[2:]
    steps = 2
    block = rows // steps
    picked = pl.BlockSpec((1, block, features), lambda i, chosen: (chosen[0], i, 0))
    layer = pl.BlockSpec((1, 1, block, features), lambda i, chosen: (0, chosen[0], i, 0))
    flat = pl.BlockSpec((block, features), lambda i, chosen: (i, 0))
    return pl.pallas_call(
        settle_kernel,
        out_shape=(
            jax.ShapeDtypeStruct(updated.shape, f32),
            jax.ShapeDtypeStruct((rows, features), f32),
            jax.ShapeDtypeStruct((rows, features), f32),
        ),
        grid_spec=pltpu.PrefetchScalarGridSpec(
            num_scalar_prefetch=1,
            grid=(steps,),
            in_specs=[flat, layer, picked, picked],
            out_specs=(layer, flat, flat),
        ),
        input_output_aliases={2: 0},
        cost_estimate=pl.CostEstimate(flops=1 << 20, bytes_accessed=2 << 20, transcendentals=0),
        compiler_params=pltpu.CompilerParams(vmem_limit_bytes=VMEM_LIMIT),
        name="settle",
    )(chosen, average, updated, outer_weight, outer_moment)


def sum_all(parts):
    terms = [parts[index].astype(f32) for index in range(parts.shape[0])]
    while len(terms) > 1:
        terms = [first + second for first, second in zip(terms[::2], terms[1::2])]
    return terms[0]


def spread(rows):
    return jnp.broadcast_to(rows.astype(bf16)[None], (SIDE,) + rows.shape)


def shift(offset):
    return [(source, (source + offset) % SIDE) for source in range(SIDE)]


swap = [(0, 1), (1, 0)]


def shards(activations, cotangent, local_weight, outer_weight, outer_moment, fragment_index):
    inputs = activations[0]
    upstream = cotangent[0]
    layers = local_weight[0]
    features = upstream.shape[1]
    chosen = fragment_index[0]
    place = jnp.stack([lax.axis_index(name) for name in ("x", "c")]).astype(jnp.int32)

    theirs = lax.ppermute(inputs, "c", swap)
    their_up = lax.ppermute(upstream, "c", swap)
    part = grad(place, inputs, theirs, upstream, their_up)
    rows = lax.all_gather(cast(layers, part), "zl", axis=0, tiled=True)
    pick = lambda array: lax.dynamic_index_in_dim(array, chosen, 0, keepdims=False)
    delta = pick(outer_weight) - pick(layers)
    part = lax.all_to_all(part, "x", 0, 0)
    part, rows, delta = lax.optimization_barrier((part, rows, delta))

    part = sum_all(part).astype(bf16).reshape(SIDE, PIECE, features)
    part = lax.all_to_all(part, "zl", 0, 0)
    weights = [rows] + [lax.ppermute(rows, "x", shift(offset)) for offset in (1, 2, 3)]

    mean = delta + jnp.where(chosen == 0, inner_rate, 0.0) * sum_all(part)
    mean = mean.astype(bf16).reshape(SIDE, QUARTER, features)
    mean = sum_all(lax.all_to_all(mean, "y", 0, 0)) * (1.0 / (SIDE * SIDE))
    mean, weights[1], weights[3] = lax.optimization_barrier((mean, weights[1], weights[3]))
    mean = sum_all(lax.all_to_all(spread(mean), "zh", 0, 0))
    mean = lax.all_to_all(spread(mean), "y", 0, 0).reshape(PIECE, features)

    updated = update(part, local_weight)
    other = lax.ppermute(their_keys(place, theirs, weights, updated), "c", swap)
    keys = own_keys(place, inputs, weights, other)
    local_new, outer_new, moment_new = settle(
        fragment_index, mean, updated, outer_weight, outer_moment
    )
    return keys, local_new, outer_new, moment_new


def solution(mesh):
    fine = Mesh(
        mesh.devices.reshape(SIDE, SIDE, SIDE, SIDE, CORES), ("zh", "y", "x", "zl", "c")
    )
    replica = ("zh", "y")
    fsdp = ("x", "zl", "c")
    in_specs = (
        P(replica, fsdp, None),
        P(replica, fsdp, None),
        P(replica, None, fsdp, None),
        P(None, fsdp, None),
        P(None, fsdp, None),
        P(),
    )
    out_specs = (
        P(replica, fsdp, None),
        P(replica, None, fsdp, None),
        P(fsdp, None),
        P(fsdp, None),
    )
    return jax.shard_map(shards, mesh=fine, in_specs=in_specs, out_specs=out_specs, check_vma=False)
```

```python
import jax
import jax.numpy as jnp
from jax import lax
from jax.experimental import pallas as pl
from jax.experimental.pallas import tpu as pltpu
from jax.sharding import Mesh, PartitionSpec as P

inner_rate = 0.25
outer_rate = 0.7
momentum_factor = 0.9
mixing = 0.5

SIDE = 4
CORES = 2
PIECE = 128
ROWS = SIDE * PIECE
QUARTER = PIECE // SIDE
SCALE = 4096 ** (-0.5)

VMEM_LIMIT = 12 << 20
GRAD_VMEM_LIMIT = 62 << 20

bf16 = jnp.bfloat16
f32 = jnp.float32


def core_columns(ref, core, chunk=0):
    runs = []
    for run in range(SIDE):
        start = ((chunk * SIDE + run) * CORES + core) * PIECE
        runs.append(ref[:, pl.ds(pl.multiple_of(start, PIECE), PIECE)])
    return jnp.concatenate(runs, axis=1)


def grad_kernel(
    place_ref, inputs_hbm, theirs_hbm, up_hbm, their_up_hbm, out_hbm, inputs, ups, out, in_sems, out_sems
):
    tokens = inputs_hbm.shape[0]
    copies = [
        pltpu.make_async_copy(inputs_hbm, inputs.at[:tokens], in_sems.at[0]),
        pltpu.make_async_copy(theirs_hbm, inputs.at[tokens:], in_sems.at[1]),
        pltpu.make_async_copy(up_hbm, ups.at[:tokens], in_sems.at[2]),
        pltpu.make_async_copy(their_up_hbm, ups.at[tokens:], in_sems.at[3]),
    ]
    for copy in copies:
        copy.start()
    for copy in copies:
        copy.wait()
    stores = []
    for chunk in range(SIDE):
        total = lax.dot_general(
            core_columns(inputs, place_ref[1], chunk),
            ups[...],
            (((0,), (0,)), ((), ())),
            preferred_element_type=f32,
        )
        out[chunk] = (total * SCALE).astype(bf16)
        stores.append(pltpu.make_async_copy(out.at[chunk], out_hbm.at[chunk], out_sems.at[chunk]))
        stores[-1].start()
    for store in stores:
        store.wait()


def grad(place, inputs, theirs, up, their_up):
    tokens, width = inputs.shape
    features = up.shape[1]
    anywhere = pl.BlockSpec(memory_space=pl.ANY)
    return pl.pallas_call(
        grad_kernel,
        out_shape=jax.ShapeDtypeStruct((SIDE, ROWS, features), bf16),
        in_specs=[pl.BlockSpec(memory_space=pltpu.SMEM)] + [anywhere] * 4,
        out_specs=anywhere,
        scratch_shapes=[
            pltpu.VMEM((2 * tokens, width), bf16),
            pltpu.VMEM((2 * tokens, features), bf16),
            pltpu.VMEM((SIDE, ROWS, features), bf16),
            pltpu.SemaphoreType.DMA((4,)),
            pltpu.SemaphoreType.DMA((SIDE,)),
        ],
        cost_estimate=pl.CostEstimate(flops=1 << 30, bytes_accessed=6 << 20, transcendentals=0),
        compiler_params=pltpu.CompilerParams(vmem_limit_bytes=GRAD_VMEM_LIMIT),
        name="gradient",
    )(place, inputs, theirs, up, their_up)


def cast_kernel(after_ref, layer_ref, out_ref):
    out_ref[...] = layer_ref[0].astype(bf16)


def cast(layers, after):
    features = layers.shape[2]
    return pl.pallas_call(
        cast_kernel,
        out_shape=jax.ShapeDtypeStruct((PIECE, features), bf16),
        grid=(1,),
        in_specs=[
            pl.BlockSpec(memory_space=pl.ANY),
            pl.BlockSpec((1, PIECE, features), lambda i: (0, 0, 0)),
        ],
        out_specs=pl.BlockSpec((PIECE, features), lambda i: (0, 0)),
        cost_estimate=pl.CostEstimate(flops=0, bytes_accessed=1 << 20, transcendentals=0),
        name="cast_weights",
    )(after, layers)


def keys_kernel(
    place_ref, inputs_hbm, theirs_hbm, w0_hbm, w1_hbm, w2_hbm, w3_hbm, own_ref, other_ref, inputs, theirs, weights, sems
):
    sources = (w0_hbm, w1_hbm, w2_hbm, w3_hbm)
    offsets = (0, 1, 3, 2)
    loads = [
        pltpu.make_async_copy(inputs_hbm, inputs, sems.at[SIDE]),
        pltpu.make_async_copy(theirs_hbm, theirs, sems.at[SIDE + 1]),
    ]
    rows = [
        pltpu.make_async_copy(sources[offset], weights.at[offset], sems.at[offset])
        for offset in range(SIDE)
    ]
    rows[0].start()
    for load in loads:
        load.start()
    for offset in offsets[1:]:
        rows[offset].start()
    for load in loads:
        load.wait()
    own = 0.0
    other = 0.0
    for offset in offsets:
        chunk = lax.rem(place_ref[0] + SIDE - offset, SIDE)
        rows[offset].wait()
        own += jnp.dot(
            core_columns(inputs, place_ref[1], chunk), weights[offset], preferred_element_type=f32
        )
        other += jnp.dot(
            core_columns(theirs, place_ref[1], chunk), weights[offset], preferred_element_type=f32
        )
    own_ref[...] = own * SCALE
    other_ref[...] = (other * SCALE).astype(bf16)


def half_keys(place, inputs, theirs, weights):
    tokens, width = inputs.shape
    rows, features = weights[0].shape
    anywhere = pl.BlockSpec(memory_space=pl.ANY)
    whole = pl.BlockSpec(memory_space=pltpu.VMEM)
    return pl.pallas_call(
        keys_kernel,
        out_shape=(
            jax.ShapeDtypeStruct((tokens, features), f32),
            jax.ShapeDtypeStruct((tokens, features), bf16),
        ),
        in_specs=[pl.BlockSpec(memory_space=pltpu.SMEM)] + [anywhere] * (2 + SIDE),
        out_specs=(whole, whole),
        scratch_shapes=[
            pltpu.VMEM((tokens, width), bf16),
            pltpu.VMEM((tokens, width), bf16),
            pltpu.VMEM((SIDE, rows, features), bf16),
            pltpu.SemaphoreType.DMA((SIDE + 2,)),
        ],
        cost_estimate=pl.CostEstimate(flops=1 << 30, bytes_accessed=7 << 20, transcendentals=0),
        compiler_params=pltpu.CompilerParams(vmem_limit_bytes=GRAD_VMEM_LIMIT),
        name="half_keys",
    )(place, inputs, theirs, *weights)


def update_kernel(gradient_ref, layers_ref, out_ref):
    out_ref[0, 0] = layers_ref[0, 0] - inner_rate * gradient_ref[...]
    for layer in range(1, layers_ref.shape[1]):
        out_ref[0, layer] = layers_ref[0, layer]


def update(gradient, local_weight):
    count, rows, features = local_weight.shape[1:]
    steps = 2
    block = rows // steps
    layers = pl.BlockSpec((1, count, block, features), lambda i: (0, 0, i, 0))
    return pl.pallas_call(
        update_kernel,
        out_shape=jax.ShapeDtypeStruct(local_weight.shape, f32),
        grid=(steps,),
        in_specs=[pl.BlockSpec((block, features), lambda i: (i, 0)), layers],
        out_specs=layers,
        cost_estimate=pl.CostEstimate(flops=1 << 19, bytes_accessed=2 << 20, transcendentals=0),
        compiler_params=pltpu.CompilerParams(vmem_limit_bytes=VMEM_LIMIT),
        name="update",
    )(gradient, local_weight)


def settle_kernel(
    chosen_ref,
    average_hbm,
    layers_hbm,
    outer_hbm,
    moment_hbm,
    layers_out,
    outer_out,
    moment_out,
    average,
    olds,
    news,
    in_sems,
    out_sems,
):
    chosen = chosen_ref[0]
    loads = [
        pltpu.make_async_copy(moment_hbm.at[chosen], olds.at[0], in_sems.at[0]),
        pltpu.make_async_copy(average_hbm, average, in_sems.at[1]),
        pltpu.make_async_copy(outer_hbm.at[chosen], olds.at[1], in_sems.at[2]),
        pltpu.make_async_copy(layers_hbm.at[0, chosen], olds.at[2], in_sems.at[3]),
    ]
    stores = [
        pltpu.make_async_copy(news.at[0], moment_out, out_sems.at[0]),
        pltpu.make_async_copy(news.at[1], outer_out, out_sems.at[1]),
        pltpu.make_async_copy(news.at[2], layers_out.at[0, chosen], out_sems.at[2]),
    ]
    for load in loads:
        load.start()
    loads[0].wait()
    loads[1].wait()
    news[0] = momentum_factor * olds[0] + average[...].astype(f32)
    stores[0].start()
    loads[2].wait()
    news[1] = olds[1] - outer_rate * (average[...].astype(f32) + momentum_factor * news[0])
    stores[1].start()
    loads[3].wait()
    news[2] = mixing * olds[2] + (1.0 - mixing) * news[1]
    stores[2].start()
    for store in stores:
        store.wait()


def settle(chosen, average, updated, outer_weight, outer_moment):
    rows, features = updated.shape[2:]
    anywhere = pl.BlockSpec(memory_space=pl.ANY)
    return pl.pallas_call(
        settle_kernel,
        out_shape=(
            jax.ShapeDtypeStruct(updated.shape, f32),
            jax.ShapeDtypeStruct((rows, features), f32),
            jax.ShapeDtypeStruct((rows, features), f32),
        ),
        in_specs=[pl.BlockSpec(memory_space=pltpu.SMEM)] + [anywhere] * 4,
        out_specs=(anywhere,) * 3,
        scratch_shapes=[
            pltpu.VMEM((rows, features), average.dtype),
            pltpu.VMEM((3, rows, features), f32),
            pltpu.VMEM((3, rows, features), f32),
            pltpu.SemaphoreType.DMA((4,)),
            pltpu.SemaphoreType.DMA((3,)),
        ],
        input_output_aliases={2: 0},
        cost_estimate=pl.CostEstimate(flops=1 << 20, bytes_accessed=2 << 20, transcendentals=0),
        compiler_params=pltpu.CompilerParams(vmem_limit_bytes=VMEM_LIMIT),
        name="settle",
    )(chosen, average, updated, outer_weight, outer_moment)


def sum_all(parts):
    terms = [parts[index].astype(f32) for index in range(parts.shape[0])]
    while len(terms) > 1:
        terms = [first + second for first, second in zip(terms[::2], terms[1::2])]
    return terms[0]


def spread(rows):
    return jnp.broadcast_to(rows.astype(bf16)[None], (SIDE,) + rows.shape)


def shift(offset):
    return [(source, (source + offset) % SIDE) for source in range(SIDE)]


swap = [(0, 1), (1, 0)]


def trained_step(activations, cotangent, local_weight, outer_weight, outer_moment, fragment_index):
    inputs = activations[0]
    upstream = cotangent[0]
    layers = local_weight[0]
    features = upstream.shape[1]
    place = jnp.stack([lax.axis_index(name) for name in ("x", "c")]).astype(jnp.int32)

    theirs = lax.ppermute(inputs, "c", swap)
    their_up = lax.ppermute(upstream, "c", swap)
    part = grad(place, inputs, theirs, upstream, their_up)
    rows = lax.all_gather(cast(layers, part), "zl", axis=0, tiled=True)
    delta = outer_weight[0] - layers[0]
    part = lax.all_to_all(part, "x", 0, 0)
    part, rows, delta = lax.optimization_barrier((part, rows, delta))

    part = sum_all(part).astype(bf16).reshape(SIDE, PIECE, features)
    part = lax.all_to_all(part, "zl", 0, 0)
    weights = [rows] + [lax.ppermute(rows, "x", shift(offset)) for offset in (1, 2, 3)]

    gradient = sum_all(part)
    mean = delta + inner_rate * gradient
    mean = mean.astype(bf16).reshape(SIDE, QUARTER, features)
    mean = sum_all(lax.all_to_all(mean, "y", 0, 0)) * (1.0 / (SIDE * SIDE))
    mean, weights[1], weights[3] = lax.optimization_barrier((mean, weights[1], weights[3]))
    mean = sum_all(lax.all_to_all(spread(mean), "zh", 0, 0))
    mean, gradient = lax.optimization_barrier((mean, gradient))
    mean = lax.all_to_all(spread(mean), "y", 0, 0).reshape(PIECE, features)

    own, other = half_keys(place, inputs, theirs, weights)
    other = lax.ppermute(other, "c", swap)
    keys = (own + other.astype(f32)).astype(bf16)[None]
    updated = update(gradient, local_weight)
    local_new, outer_new, moment_new = settle(
        fragment_index, mean, updated, outer_weight, outer_moment
    )
    return keys, local_new, outer_new, moment_new


def flip(mask):
    return [(source, source ^ mask) for source in range(SIDE)]


def other_step(activations, cotangent, local_weight, outer_weight, outer_moment, fragment_index):
    inputs = activations[0]
    upstream = cotangent[0]
    layers = local_weight[0]
    features = upstream.shape[1]
    place = jnp.stack([lax.axis_index(name) for name in ("x", "c")]).astype(jnp.int32)

    theirs = lax.ppermute(inputs, "c", swap)
    their_up = lax.ppermute(upstream, "c", swap)
    part = grad(place, inputs, theirs, upstream, their_up)
    rows = lax.all_gather(cast(layers, part), "zl", axis=0, tiled=True)
    pick = lambda array: lax.dynamic_index_in_dim(array, fragment_index[0], 0, keepdims=False)
    delta = (pick(outer_weight) - pick(layers)).astype(bf16).reshape(SIDE, QUARTER, features)
    part = lax.all_to_all(part, "x", 0, 0)
    part, rows, delta = lax.optimization_barrier((part, rows, delta))
    weights = [rows] + [lax.ppermute(rows, "x", shift(offset)) for offset in (1, 2, 3)]

    mean = sum_all(lax.all_to_all(delta, "y", 0, 0)) * (1.0 / (SIDE * SIDE))
    part = sum_all(part).astype(bf16).reshape(SIDE, PIECE, features)
    mean = sum_all(lax.all_to_all(spread(mean), "zh", 0, 0))
    mean = lax.all_to_all(spread(mean), "y", 0, 0).reshape(PIECE, features)

    along = lax.axis_index("zl")
    chunk = lambda mask: lax.dynamic_index_in_dim(part, along ^ mask, 0, keepdims=False)
    gradient = sum_all(
        jnp.stack([chunk(0)] + [lax.ppermute(chunk(mask), "zl", flip(mask)) for mask in (1, 2, 3)])
    )

    own, other = half_keys(place, inputs, theirs, weights)
    other = lax.ppermute(other, "c", swap)
    keys = (own + other.astype(f32)).astype(bf16)[None]
    updated = update(gradient, local_weight)
    local_new, outer_new, moment_new = settle(
        fragment_index, mean, updated, outer_weight, outer_moment
    )
    return keys, local_new, outer_new, moment_new


def shards(activations, cotangent, local_weight, outer_weight, outer_moment, fragment_index):
    return lax.cond(
        fragment_index[0] == 0,
        trained_step,
        other_step,
        activations,
        cotangent,
        local_weight,
        outer_weight,
        outer_moment,
        fragment_index,
    )


def solution(mesh):
    fine = Mesh(
        mesh.devices.reshape(SIDE, SIDE, SIDE, SIDE, CORES), ("zh", "y", "x", "zl", "c")
    )
    replica = ("zh", "y")
    fsdp = ("x", "zl", "c")
    in_specs = (
        P(replica, fsdp, None),
        P(replica, fsdp, None),
        P(replica, None, fsdp, None),
        P(None, fsdp, None),
        P(None, fsdp, None),
        P(),
    )
    out_specs = (
        P(replica, fsdp, None),
        P(replica, None, fsdp, None),
        P(fsdp, None),
        P(fsdp, None),
    )
    return jax.shard_map(shards, mesh=fine, in_specs=in_specs, out_specs=out_specs, check_vma=False)
```

```python
import jax
import jax.numpy as jnp
from jax import lax
from jax.experimental import pallas as pl
from jax.experimental.pallas import tpu as pltpu
from jax.sharding import Mesh, PartitionSpec as P

inner_rate = 0.25
outer_rate = 0.7
momentum_factor = 0.9
mixing = 0.5

SIDE = 4
CORES = 2
PIECE = 128
ROWS = SIDE * PIECE
QUARTER = PIECE // SIDE
SCALE = 4096 ** (-0.5)

VMEM_LIMIT = 12 << 20
GRAD_VMEM_LIMIT = 62 << 20
KEYS_VMEM_LIMIT = 24 << 20

bf16 = jnp.bfloat16
f32 = jnp.float32


def core_columns(ref, core, chunk=0):
    runs = []
    for run in range(SIDE):
        start = ((chunk * SIDE + run) * CORES + core) * PIECE
        runs.append(ref[:, pl.ds(pl.multiple_of(start, PIECE), PIECE)])
    return jnp.concatenate(runs, axis=1)


def grad_kernel(
    place_ref, inputs_hbm, theirs_hbm, up_hbm, their_up_hbm, out_hbm, inputs, ups, out, in_sems, out_sems
):
    tokens = inputs_hbm.shape[0]
    copies = [
        pltpu.make_async_copy(inputs_hbm, inputs.at[:tokens], in_sems.at[0]),
        pltpu.make_async_copy(theirs_hbm, inputs.at[tokens:], in_sems.at[1]),
        pltpu.make_async_copy(up_hbm, ups.at[:tokens], in_sems.at[2]),
        pltpu.make_async_copy(their_up_hbm, ups.at[tokens:], in_sems.at[3]),
    ]
    for copy in copies:
        copy.start()
    for copy in copies:
        copy.wait()
    stores = []
    for chunk in range(SIDE):
        total = lax.dot_general(
            core_columns(inputs, place_ref[1], chunk),
            ups[...],
            (((0,), (0,)), ((), ())),
            preferred_element_type=f32,
        )
        out[chunk] = (total * SCALE).astype(bf16)
        stores.append(pltpu.make_async_copy(out.at[chunk], out_hbm.at[chunk], out_sems.at[chunk]))
        stores[-1].start()
    for store in stores:
        store.wait()


def grad(place, inputs, theirs, up, their_up):
    tokens, width = inputs.shape
    features = up.shape[1]
    anywhere = pl.BlockSpec(memory_space=pl.ANY)
    return pl.pallas_call(
        grad_kernel,
        out_shape=jax.ShapeDtypeStruct((SIDE, ROWS, features), bf16),
        in_specs=[pl.BlockSpec(memory_space=pltpu.SMEM)] + [anywhere] * 4,
        out_specs=anywhere,
        scratch_shapes=[
            pltpu.VMEM((2 * tokens, width), bf16),
            pltpu.VMEM((2 * tokens, features), bf16),
            pltpu.VMEM((SIDE, ROWS, features), bf16),
            pltpu.SemaphoreType.DMA((4,)),
            pltpu.SemaphoreType.DMA((SIDE,)),
        ],
        cost_estimate=pl.CostEstimate(flops=1 << 30, bytes_accessed=6 << 20, transcendentals=0),
        compiler_params=pltpu.CompilerParams(vmem_limit_bytes=GRAD_VMEM_LIMIT),
        name="gradient",
    )(place, inputs, theirs, up, their_up)


def cast_kernel(after_ref, layer_ref, out_ref):
    out_ref[...] = layer_ref[0].astype(bf16)


def cast(layers, after):
    features = layers.shape[2]
    return pl.pallas_call(
        cast_kernel,
        out_shape=jax.ShapeDtypeStruct((PIECE, features), bf16),
        grid=(1,),
        in_specs=[
            pl.BlockSpec(memory_space=pl.ANY),
            pl.BlockSpec((1, PIECE, features), lambda i: (0, 0, 0)),
        ],
        out_specs=pl.BlockSpec((PIECE, features), lambda i: (0, 0)),
        cost_estimate=pl.CostEstimate(flops=0, bytes_accessed=1 << 20, transcendentals=0),
        name="cast_weights",
    )(after, layers)


def keys_kernel(
    place_ref, inputs_hbm, theirs_hbm, w0_hbm, w1_hbm, w2_hbm, w3_hbm, own_ref, other_ref, inputs, theirs, weights, sems
):
    sources = (w0_hbm, w1_hbm, w2_hbm, w3_hbm)
    offsets = (0, 1, 3, 2)
    loads = [
        pltpu.make_async_copy(inputs_hbm, inputs, sems.at[SIDE]),
        pltpu.make_async_copy(theirs_hbm, theirs, sems.at[SIDE + 1]),
    ]
    rows = [
        pltpu.make_async_copy(sources[offset], weights.at[offset], sems.at[offset])
        for offset in range(SIDE)
    ]
    rows[0].start()
    for load in loads:
        load.start()
    for offset in offsets[1:]:
        rows[offset].start()
    for load in loads:
        load.wait()
    own = 0.0
    other = 0.0
    for offset in offsets:
        chunk = lax.rem(place_ref[0] + SIDE - offset, SIDE)
        rows[offset].wait()
        own += jnp.dot(
            core_columns(inputs, place_ref[1], chunk), weights[offset], preferred_element_type=f32
        )
        other += jnp.dot(
            core_columns(theirs, place_ref[1], chunk), weights[offset], preferred_element_type=f32
        )
    own_ref[...] = own * SCALE
    other_ref[...] = (other * SCALE).astype(bf16)


def half_keys(place, inputs, theirs, weights):
    tokens, width = inputs.shape
    rows, features = weights[0].shape
    anywhere = pl.BlockSpec(memory_space=pl.ANY)
    whole = pl.BlockSpec(memory_space=pltpu.VMEM)
    return pl.pallas_call(
        keys_kernel,
        out_shape=(
            jax.ShapeDtypeStruct((tokens, features), f32),
            jax.ShapeDtypeStruct((tokens, features), bf16),
        ),
        in_specs=[pl.BlockSpec(memory_space=pltpu.SMEM)] + [anywhere] * (2 + SIDE),
        out_specs=(whole, whole),
        scratch_shapes=[
            pltpu.VMEM((tokens, width), bf16),
            pltpu.VMEM((tokens, width), bf16),
            pltpu.VMEM((SIDE, rows, features), bf16),
            pltpu.SemaphoreType.DMA((SIDE + 2,)),
        ],
        cost_estimate=pl.CostEstimate(flops=1 << 30, bytes_accessed=7 << 20, transcendentals=0),
        compiler_params=pltpu.CompilerParams(vmem_limit_bytes=KEYS_VMEM_LIMIT),
        name="half_keys",
    )(place, inputs, theirs, *weights)


def update_kernel(gradient_ref, layers_ref, own_ref, other_ref, out_ref, keys_ref):
    out_ref[0, 0] = layers_ref[0, 0] - inner_rate * gradient_ref[...]
    for layer in range(1, layers_ref.shape[1]):
        out_ref[0, layer] = layers_ref[0, layer]
    keys_ref[0] = (own_ref[...] + other_ref[...].astype(f32)).astype(bf16)


def update(gradient, local_weight, own, other):
    count, rows, features = local_weight.shape[1:]
    tokens = own.shape[0]
    steps = 2
    block = rows // steps
    layers = pl.BlockSpec((1, count, block, features), lambda i: (0, 0, i, 0))
    half = pl.BlockSpec((tokens // steps, features), lambda i: (i, 0))
    return pl.pallas_call(
        update_kernel,
        out_shape=(
            jax.ShapeDtypeStruct(local_weight.shape, f32),
            jax.ShapeDtypeStruct((1, tokens, features), bf16),
        ),
        grid=(steps,),
        in_specs=[pl.BlockSpec((block, features), lambda i: (i, 0)), layers, half, half],
        out_specs=(layers, pl.BlockSpec((1, tokens // steps, features), lambda i: (0, i, 0))),
        cost_estimate=pl.CostEstimate(flops=1 << 19, bytes_accessed=3 << 20, transcendentals=0),
        compiler_params=pltpu.CompilerParams(vmem_limit_bytes=VMEM_LIMIT),
        name="update",
    )(gradient, local_weight, own, other)


def settle_kernel(
    chosen_ref,
    average_hbm,
    layers_hbm,
    outer_hbm,
    moment_hbm,
    layers_out,
    outer_out,
    moment_out,
    average,
    olds,
    news,
    in_sems,
    out_sems,
):
    chosen = chosen_ref[0]
    loads = [
        pltpu.make_async_copy(moment_hbm.at[chosen], olds.at[0], in_sems.at[0]),
        pltpu.make_async_copy(average_hbm, average, in_sems.at[1]),
        pltpu.make_async_copy(outer_hbm.at[chosen], olds.at[1], in_sems.at[2]),
        pltpu.make_async_copy(layers_hbm.at[0, chosen], olds.at[2], in_sems.at[3]),
    ]
    stores = [
        pltpu.make_async_copy(news.at[0], moment_out, out_sems.at[0]),
        pltpu.make_async_copy(news.at[1], outer_out, out_sems.at[1]),
        pltpu.make_async_copy(news.at[2], layers_out.at[0, chosen], out_sems.at[2]),
    ]
    for load in loads:
        load.start()
    loads[0].wait()
    loads[1].wait()
    news[0] = momentum_factor * olds[0] + average[...].astype(f32)
    stores[0].start()
    loads[2].wait()
    news[1] = olds[1] - outer_rate * (average[...].astype(f32) + momentum_factor * news[0])
    stores[1].start()
    loads[3].wait()
    news[2] = mixing * olds[2] + (1.0 - mixing) * news[1]
    stores[2].start()
    for store in stores:
        store.wait()


def settle(chosen, average, updated, outer_weight, outer_moment):
    rows, features = updated.shape[2:]
    anywhere = pl.BlockSpec(memory_space=pl.ANY)
    return pl.pallas_call(
        settle_kernel,
        out_shape=(
            jax.ShapeDtypeStruct(updated.shape, f32),
            jax.ShapeDtypeStruct((rows, features), f32),
            jax.ShapeDtypeStruct((rows, features), f32),
        ),
        in_specs=[pl.BlockSpec(memory_space=pltpu.SMEM)] + [anywhere] * 4,
        out_specs=(anywhere,) * 3,
        scratch_shapes=[
            pltpu.VMEM((rows, features), average.dtype),
            pltpu.VMEM((3, rows, features), f32),
            pltpu.VMEM((3, rows, features), f32),
            pltpu.SemaphoreType.DMA((4,)),
            pltpu.SemaphoreType.DMA((3,)),
        ],
        input_output_aliases={2: 0},
        cost_estimate=pl.CostEstimate(flops=1 << 20, bytes_accessed=2 << 20, transcendentals=0),
        compiler_params=pltpu.CompilerParams(vmem_limit_bytes=VMEM_LIMIT),
        name="settle",
    )(chosen, average, updated, outer_weight, outer_moment)


def sum_all(parts):
    terms = [parts[index].astype(f32) for index in range(parts.shape[0])]
    while len(terms) > 1:
        terms = [first + second for first, second in zip(terms[::2], terms[1::2])]
    return terms[0]


def spread(rows):
    return jnp.broadcast_to(rows.astype(bf16)[None], (SIDE,) + rows.shape)


def shift(offset):
    return [(source, (source + offset) % SIDE) for source in range(SIDE)]


swap = [(0, 1), (1, 0)]


def trained_step(activations, cotangent, local_weight, outer_weight, outer_moment, fragment_index):
    inputs = activations[0]
    upstream = cotangent[0]
    layers = local_weight[0]
    features = upstream.shape[1]
    place = jnp.stack([lax.axis_index(name) for name in ("x", "c")]).astype(jnp.int32)

    theirs = lax.ppermute(inputs, "c", swap)
    their_up = lax.ppermute(upstream, "c", swap)
    part = grad(place, inputs, theirs, upstream, their_up)
    rows = lax.all_gather(cast(layers, part), "zl", axis=0, tiled=True)
    delta = outer_weight[0] - layers[0]
    part = lax.all_to_all(part, "x", 0, 0)
    part, rows, delta = lax.optimization_barrier((part, rows, delta))

    part = sum_all(part).astype(bf16).reshape(SIDE, PIECE, features)
    part = lax.all_to_all(part, "zl", 0, 0)
    weights = [rows] + [lax.ppermute(rows, "x", shift(offset)) for offset in (1, 2, 3)]

    gradient = sum_all(part)
    mean = delta + inner_rate * gradient
    mean = mean.astype(bf16).reshape(SIDE, QUARTER, features)
    mean = sum_all(lax.all_to_all(mean, "y", 0, 0)) * (1.0 / (SIDE * SIDE))
    mean, weights[1], weights[3] = lax.optimization_barrier((mean, weights[1], weights[3]))
    mean = sum_all(lax.all_to_all(spread(mean), "zh", 0, 0))
    mean, gradient = lax.optimization_barrier((mean, gradient))
    mean = lax.all_to_all(spread(mean), "y", 0, 0).reshape(PIECE, features)

    own, other = half_keys(place, inputs, theirs, weights)
    other = lax.ppermute(other, "c", swap)
    updated, keys = update(gradient, local_weight, own, other)
    local_new, outer_new, moment_new = settle(
        fragment_index, mean, updated, outer_weight, outer_moment
    )
    return keys, local_new, outer_new, moment_new


def flip(mask):
    return [(source, source ^ mask) for source in range(SIDE)]


def other_step(activations, cotangent, local_weight, outer_weight, outer_moment, fragment_index):
    inputs = activations[0]
    upstream = cotangent[0]
    layers = local_weight[0]
    features = upstream.shape[1]
    place = jnp.stack([lax.axis_index(name) for name in ("x", "c")]).astype(jnp.int32)

    theirs = lax.ppermute(inputs, "c", swap)
    their_up = lax.ppermute(upstream, "c", swap)
    part = grad(place, inputs, theirs, upstream, their_up)
    rows = lax.all_gather(cast(layers, part), "zl", axis=0, tiled=True)
    pick = lambda array: lax.dynamic_index_in_dim(array, fragment_index[0], 0, keepdims=False)
    delta = (pick(outer_weight) - pick(layers)).astype(bf16).reshape(SIDE, QUARTER, features)
    part = lax.all_to_all(part, "x", 0, 0)
    part, rows, delta = lax.optimization_barrier((part, rows, delta))
    weights = [rows] + [lax.ppermute(rows, "x", shift(offset)) for offset in (1, 2, 3)]

    mean = sum_all(lax.all_to_all(delta, "y", 0, 0)) * (1.0 / (SIDE * SIDE))
    part = sum_all(part).astype(bf16).reshape(SIDE, PIECE, features)
    mean = sum_all(lax.all_to_all(spread(mean), "zh", 0, 0))
    mean = lax.all_to_all(spread(mean), "y", 0, 0).reshape(PIECE, features)

    along = lax.axis_index("zl")
    chunk = lambda mask: lax.dynamic_index_in_dim(part, along ^ mask, 0, keepdims=False)
    gradient = sum_all(
        jnp.stack([chunk(0)] + [lax.ppermute(chunk(mask), "zl", flip(mask)) for mask in (1, 2, 3)])
    )

    own, other = half_keys(place, inputs, theirs, weights)
    other = lax.ppermute(other, "c", swap)
    updated, keys = update(gradient, local_weight, own, other)
    local_new, outer_new, moment_new = settle(
        fragment_index, mean, updated, outer_weight, outer_moment
    )
    return keys, local_new, outer_new, moment_new


def shards(activations, cotangent, local_weight, outer_weight, outer_moment, fragment_index):
    return lax.cond(
        fragment_index[0] == 0,
        trained_step,
        other_step,
        activations,
        cotangent,
        local_weight,
        outer_weight,
        outer_moment,
        fragment_index,
    )


def solution(mesh):
    fine = Mesh(
        mesh.devices.reshape(SIDE, SIDE, SIDE, SIDE, CORES), ("zh", "y", "x", "zl", "c")
    )
    replica = ("zh", "y")
    fsdp = ("x", "zl", "c")
    in_specs = (
        P(replica, fsdp, None),
        P(replica, fsdp, None),
        P(replica, None, fsdp, None),
        P(None, fsdp, None),
        P(None, fsdp, None),
        P(),
    )
    out_specs = (
        P(replica, fsdp, None),
        P(replica, None, fsdp, None),
        P(fsdp, None),
        P(fsdp, None),
    )
    return jax.shard_map(shards, mesh=fine, in_specs=in_specs, out_specs=out_specs, check_vma=False)
```

```python
import jax
import jax.numpy as jnp
from jax import lax
from jax.experimental import pallas as pl
from jax.experimental.pallas import tpu as pltpu
from jax.sharding import Mesh, PartitionSpec as P

inner_rate = 0.25
outer_rate = 0.7
momentum_factor = 0.9
mixing = 0.5

SIDE = 4
CORES = 2
PIECE = 128
ROWS = SIDE * PIECE
QUARTER = PIECE // SIDE
SCALE = 4096 ** (-0.5)

VMEM_LIMIT = 12 << 20
GRAD_VMEM_LIMIT = 62 << 20
KEYS_VMEM_LIMIT = 24 << 20

bf16 = jnp.bfloat16
f32 = jnp.float32


def core_columns(ref, core, chunk=0):
    runs = []
    for run in range(SIDE):
        start = ((chunk * SIDE + run) * CORES + core) * PIECE
        runs.append(ref[:, pl.ds(pl.multiple_of(start, PIECE), PIECE)])
    return jnp.concatenate(runs, axis=1)


def grad_kernel(
    place_ref, inputs_hbm, theirs_hbm, up_hbm, their_up_hbm, out_hbm, inputs, ups, out, in_sems, out_sems
):
    tokens = inputs_hbm.shape[0]
    copies = [
        pltpu.make_async_copy(inputs_hbm, inputs.at[:tokens], in_sems.at[0]),
        pltpu.make_async_copy(theirs_hbm, inputs.at[tokens:], in_sems.at[1]),
        pltpu.make_async_copy(up_hbm, ups.at[:tokens], in_sems.at[2]),
        pltpu.make_async_copy(their_up_hbm, ups.at[tokens:], in_sems.at[3]),
    ]
    for copy in copies:
        copy.start()
    for copy in copies:
        copy.wait()
    stores = []
    for chunk in range(SIDE):
        total = lax.dot_general(
            core_columns(inputs, place_ref[1], chunk),
            ups[...],
            (((0,), (0,)), ((), ())),
            preferred_element_type=f32,
        )
        out[chunk] = (total * SCALE).astype(bf16)
        stores.append(pltpu.make_async_copy(out.at[chunk], out_hbm.at[chunk], out_sems.at[chunk]))
        stores[-1].start()
    for store in stores:
        store.wait()


def grad(place, inputs, theirs, up, their_up):
    tokens, width = inputs.shape
    features = up.shape[1]
    anywhere = pl.BlockSpec(memory_space=pl.ANY)
    return pl.pallas_call(
        grad_kernel,
        out_shape=jax.ShapeDtypeStruct((SIDE, ROWS, features), bf16),
        in_specs=[pl.BlockSpec(memory_space=pltpu.SMEM)] + [anywhere] * 4,
        out_specs=anywhere,
        scratch_shapes=[
            pltpu.VMEM((2 * tokens, width), bf16),
            pltpu.VMEM((2 * tokens, features), bf16),
            pltpu.VMEM((SIDE, ROWS, features), bf16),
            pltpu.SemaphoreType.DMA((4,)),
            pltpu.SemaphoreType.DMA((SIDE,)),
        ],
        cost_estimate=pl.CostEstimate(flops=1 << 30, bytes_accessed=6 << 20, transcendentals=0),
        compiler_params=pltpu.CompilerParams(vmem_limit_bytes=GRAD_VMEM_LIMIT),
        name="gradient",
    )(place, inputs, theirs, up, their_up)


def cast_kernel(after_ref, layer_ref, out_ref):
    out_ref[...] = layer_ref[0].astype(bf16)


def cast(layers, after):
    features = layers.shape[2]
    return pl.pallas_call(
        cast_kernel,
        out_shape=jax.ShapeDtypeStruct((PIECE, features), bf16),
        grid=(1,),
        in_specs=[
            pl.BlockSpec(memory_space=pl.ANY),
            pl.BlockSpec((1, PIECE, features), lambda i: (0, 0, 0)),
        ],
        out_specs=pl.BlockSpec((PIECE, features), lambda i: (0, 0)),
        cost_estimate=pl.CostEstimate(flops=0, bytes_accessed=1 << 20, transcendentals=0),
        name="cast_weights",
    )(after, layers)


def keys_kernel(
    place_ref, inputs_hbm, theirs_hbm, w0_hbm, w1_hbm, w2_hbm, w3_hbm, own_ref, other_ref, inputs, theirs, weights, sems
):
    sources = (w0_hbm, w1_hbm, w2_hbm, w3_hbm)
    offsets = (0, 1, 3, 2)
    loads = [
        pltpu.make_async_copy(inputs_hbm, inputs, sems.at[SIDE]),
        pltpu.make_async_copy(theirs_hbm, theirs, sems.at[SIDE + 1]),
    ]
    rows = [
        pltpu.make_async_copy(sources[offset], weights.at[offset], sems.at[offset])
        for offset in range(SIDE)
    ]
    rows[0].start()
    for load in loads:
        load.start()
    for offset in offsets[1:]:
        rows[offset].start()
    for load in loads:
        load.wait()
    own = 0.0
    other = 0.0
    for offset in offsets:
        chunk = lax.rem(place_ref[0] + SIDE - offset, SIDE)
        rows[offset].wait()
        own += jnp.dot(
            core_columns(inputs, place_ref[1], chunk), weights[offset], preferred_element_type=f32
        )
        other += jnp.dot(
            core_columns(theirs, place_ref[1], chunk), weights[offset], preferred_element_type=f32
        )
    own_ref[...] = own * SCALE
    other_ref[...] = (other * SCALE).astype(bf16)


def half_keys(place, inputs, theirs, weights):
    tokens, width = inputs.shape
    rows, features = weights[0].shape
    anywhere = pl.BlockSpec(memory_space=pl.ANY)
    whole = pl.BlockSpec(memory_space=pltpu.VMEM)
    return pl.pallas_call(
        keys_kernel,
        out_shape=(
            jax.ShapeDtypeStruct((tokens, features), f32),
            jax.ShapeDtypeStruct((tokens, features), bf16),
        ),
        in_specs=[pl.BlockSpec(memory_space=pltpu.SMEM)] + [anywhere] * (2 + SIDE),
        out_specs=(whole, whole),
        scratch_shapes=[
            pltpu.VMEM((tokens, width), bf16),
            pltpu.VMEM((tokens, width), bf16),
            pltpu.VMEM((SIDE, rows, features), bf16),
            pltpu.SemaphoreType.DMA((SIDE + 2,)),
        ],
        cost_estimate=pl.CostEstimate(flops=1 << 30, bytes_accessed=7 << 20, transcendentals=0),
        compiler_params=pltpu.CompilerParams(vmem_limit_bytes=KEYS_VMEM_LIMIT),
        name="half_keys",
    )(place, inputs, theirs, *weights)


def update_kernel(layers_ref, own_ref, other_ref, *refs):
    out_ref, keys_ref = refs[-2:]
    terms = [ref[...].astype(f32) for ref in refs[:-2]]
    while len(terms) > 1:
        terms = [first + second for first, second in zip(terms[::2], terms[1::2])]
    out_ref[0, 0] = layers_ref[0, 0] - inner_rate * terms[0]
    for layer in range(1, layers_ref.shape[1]):
        out_ref[0, layer] = layers_ref[0, layer]
    keys_ref[0] = (own_ref[...] + other_ref[...].astype(f32)).astype(bf16)


def update(pieces, local_weight, own, other):
    count, rows, features = local_weight.shape[1:]
    tokens = own.shape[0]
    steps = 2
    block = rows // steps
    layers = pl.BlockSpec((1, count, block, features), lambda i: (0, 0, i, 0))
    half = pl.BlockSpec((tokens // steps, features), lambda i: (i, 0))
    return pl.pallas_call(
        update_kernel,
        out_shape=(
            jax.ShapeDtypeStruct(local_weight.shape, f32),
            jax.ShapeDtypeStruct((1, tokens, features), bf16),
        ),
        grid=(steps,),
        in_specs=[layers, half, half]
        + [pl.BlockSpec((block, features), lambda i: (i, 0))] * len(pieces),
        out_specs=(layers, pl.BlockSpec((1, tokens // steps, features), lambda i: (0, i, 0))),
        cost_estimate=pl.CostEstimate(flops=1 << 19, bytes_accessed=3 << 20, transcendentals=0),
        compiler_params=pltpu.CompilerParams(vmem_limit_bytes=VMEM_LIMIT),
        name="update",
    )(local_weight, own, other, *pieces)


def settle_kernel(
    chosen_ref,
    average_hbm,
    layers_hbm,
    outer_hbm,
    moment_hbm,
    layers_out,
    outer_out,
    moment_out,
    average,
    olds,
    news,
    in_sems,
    out_sems,
):
    chosen = chosen_ref[0]
    loads = [
        pltpu.make_async_copy(moment_hbm.at[chosen], olds.at[0], in_sems.at[0]),
        pltpu.make_async_copy(average_hbm, average, in_sems.at[1]),
        pltpu.make_async_copy(outer_hbm.at[chosen], olds.at[1], in_sems.at[2]),
        pltpu.make_async_copy(layers_hbm.at[0, chosen], olds.at[2], in_sems.at[3]),
    ]
    stores = [
        pltpu.make_async_copy(news.at[0], moment_out, out_sems.at[0]),
        pltpu.make_async_copy(news.at[1], outer_out, out_sems.at[1]),
        pltpu.make_async_copy(news.at[2], layers_out.at[0, chosen], out_sems.at[2]),
    ]
    for load in loads:
        load.start()
    loads[0].wait()
    loads[1].wait()
    news[0] = momentum_factor * olds[0] + average[...].astype(f32)
    stores[0].start()
    loads[2].wait()
    news[1] = olds[1] - outer_rate * (average[...].astype(f32) + momentum_factor * news[0])
    stores[1].start()
    loads[3].wait()
    news[2] = mixing * olds[2] + (1.0 - mixing) * news[1]
    stores[2].start()
    for store in stores:
        store.wait()


def settle(chosen, average, updated, outer_weight, outer_moment):
    rows, features = updated.shape[2:]
    anywhere = pl.BlockSpec(memory_space=pl.ANY)
    return pl.pallas_call(
        settle_kernel,
        out_shape=(
            jax.ShapeDtypeStruct(updated.shape, f32),
            jax.ShapeDtypeStruct((rows, features), f32),
            jax.ShapeDtypeStruct((rows, features), f32),
        ),
        in_specs=[pl.BlockSpec(memory_space=pltpu.SMEM)] + [anywhere] * 4,
        out_specs=(anywhere,) * 3,
        scratch_shapes=[
            pltpu.VMEM((rows, features), average.dtype),
            pltpu.VMEM((3, rows, features), f32),
            pltpu.VMEM((3, rows, features), f32),
            pltpu.SemaphoreType.DMA((4,)),
            pltpu.SemaphoreType.DMA((3,)),
        ],
        input_output_aliases={2: 0},
        cost_estimate=pl.CostEstimate(flops=1 << 20, bytes_accessed=2 << 20, transcendentals=0),
        compiler_params=pltpu.CompilerParams(vmem_limit_bytes=VMEM_LIMIT),
        name="settle",
    )(chosen, average, updated, outer_weight, outer_moment)


def sum_all(parts):
    terms = [parts[index].astype(f32) for index in range(parts.shape[0])]
    while len(terms) > 1:
        terms = [first + second for first, second in zip(terms[::2], terms[1::2])]
    return terms[0]


def spread(rows):
    return jnp.broadcast_to(rows.astype(bf16)[None], (SIDE,) + rows.shape)


def shift(offset):
    return [(source, (source + offset) % SIDE) for source in range(SIDE)]


swap = [(0, 1), (1, 0)]


def trained_step(activations, cotangent, local_weight, outer_weight, outer_moment, fragment_index):
    inputs = activations[0]
    upstream = cotangent[0]
    layers = local_weight[0]
    features = upstream.shape[1]
    place = jnp.stack([lax.axis_index(name) for name in ("x", "c")]).astype(jnp.int32)

    theirs = lax.ppermute(inputs, "c", swap)
    their_up = lax.ppermute(upstream, "c", swap)
    part = grad(place, inputs, theirs, upstream, their_up)
    rows = lax.all_gather(cast(layers, part), "zl", axis=0, tiled=True)
    delta = outer_weight[0] - layers[0]
    part = lax.all_to_all(part, "x", 0, 0)
    part, rows, delta = lax.optimization_barrier((part, rows, delta))

    part = sum_all(part).astype(bf16).reshape(SIDE, PIECE, features)
    part = lax.all_to_all(part, "zl", 0, 0)
    weights = [rows] + [lax.ppermute(rows, "x", shift(offset)) for offset in (1, 2, 3)]

    gradient = sum_all(part)
    mean = delta + inner_rate * gradient
    mean = mean.astype(bf16).reshape(SIDE, QUARTER, features)
    mean = sum_all(lax.all_to_all(mean, "y", 0, 0)) * (1.0 / (SIDE * SIDE))
    mean, weights[1], weights[3] = lax.optimization_barrier((mean, weights[1], weights[3]))
    mean = sum_all(lax.all_to_all(spread(mean), "zh", 0, 0))
    mean, gradient = lax.optimization_barrier((mean, gradient))
    mean = lax.all_to_all(spread(mean), "y", 0, 0).reshape(PIECE, features)

    own, other = half_keys(place, inputs, theirs, weights)
    other = lax.ppermute(other, "c", swap)
    updated, keys = update([gradient], local_weight, own, other)
    local_new, outer_new, moment_new = settle(
        fragment_index, mean, updated, outer_weight, outer_moment
    )
    return keys, local_new, outer_new, moment_new


def flip(mask):
    return [(source, source ^ mask) for source in range(SIDE)]


def other_step(activations, cotangent, local_weight, outer_weight, outer_moment, fragment_index):
    inputs = activations[0]
    upstream = cotangent[0]
    layers = local_weight[0]
    features = upstream.shape[1]
    place = jnp.stack([lax.axis_index(name) for name in ("x", "c")]).astype(jnp.int32)

    theirs = lax.ppermute(inputs, "c", swap)
    their_up = lax.ppermute(upstream, "c", swap)
    part = grad(place, inputs, theirs, upstream, their_up)
    rows = lax.all_gather(cast(layers, part), "zl", axis=0, tiled=True)
    pick = lambda array: lax.dynamic_index_in_dim(array, fragment_index[0], 0, keepdims=False)
    delta = (pick(outer_weight) - pick(layers)).astype(bf16).reshape(SIDE, QUARTER, features)
    part = lax.all_to_all(part, "x", 0, 0)
    part, rows, delta = lax.optimization_barrier((part, rows, delta))
    weights = [rows] + [lax.ppermute(rows, "x", shift(offset)) for offset in (1, 2, 3)]

    mean = sum_all(lax.all_to_all(delta, "y", 0, 0)) * (1.0 / (SIDE * SIDE))
    part = sum_all(part).astype(bf16).reshape(SIDE, PIECE, features)
    mean = sum_all(lax.all_to_all(spread(mean), "zh", 0, 0))
    mean = lax.all_to_all(spread(mean), "y", 0, 0).reshape(PIECE, features)

    along = lax.axis_index("zl")
    chunk = lambda mask: lax.dynamic_index_in_dim(part, along ^ mask, 0, keepdims=False)
    pieces = [chunk(0)] + [lax.ppermute(chunk(mask), "zl", flip(mask)) for mask in (1, 2, 3)]

    own, other = half_keys(place, inputs, theirs, weights)
    other = lax.ppermute(other, "c", swap)
    updated, keys = update(pieces, local_weight, own, other)
    local_new, outer_new, moment_new = settle(
        fragment_index, mean, updated, outer_weight, outer_moment
    )
    return keys, local_new, outer_new, moment_new


def shards(activations, cotangent, local_weight, outer_weight, outer_moment, fragment_index):
    return lax.cond(
        fragment_index[0] == 0,
        trained_step,
        other_step,
        activations,
        cotangent,
        local_weight,
        outer_weight,
        outer_moment,
        fragment_index,
    )


def solution(mesh):
    fine = Mesh(
        mesh.devices.reshape(SIDE, SIDE, SIDE, SIDE, CORES), ("zh", "y", "x", "zl", "c")
    )
    replica = ("zh", "y")
    fsdp = ("x", "zl", "c")
    in_specs = (
        P(replica, fsdp, None),
        P(replica, fsdp, None),
        P(replica, None, fsdp, None),
        P(None, fsdp, None),
        P(None, fsdp, None),
        P(),
    )
    out_specs = (
        P(replica, fsdp, None),
        P(replica, None, fsdp, None),
        P(fsdp, None),
        P(fsdp, None),
    )
    return jax.shard_map(shards, mesh=fine, in_specs=in_specs, out_specs=out_specs, check_vma=False)
```

```python
import jax
import jax.numpy as jnp
from jax import lax
from jax.experimental import pallas as pl
from jax.experimental.pallas import tpu as pltpu
from jax.sharding import Mesh, PartitionSpec as P

inner_rate = 0.25
outer_rate = 0.7
momentum_factor = 0.9
mixing = 0.5

SIDE = 4
CORES = 2
PIECE = 128
ROWS = SIDE * PIECE
QUARTER = PIECE // SIDE
SCALE = 4096 ** (-0.5)

VMEM_LIMIT = 12 << 20
GRAD_VMEM_LIMIT = 62 << 20
KEYS_VMEM_LIMIT = 24 << 20

bf16 = jnp.bfloat16
f32 = jnp.float32


def core_columns(ref, core, chunk=0):
    runs = []
    for run in range(SIDE):
        start = ((chunk * SIDE + run) * CORES + core) * PIECE
        runs.append(ref[:, pl.ds(pl.multiple_of(start, PIECE), PIECE)])
    return jnp.concatenate(runs, axis=1)


def grad_kernel(
    place_ref, inputs_hbm, theirs_hbm, up_hbm, their_up_hbm, out_hbm, inputs, ups, out, in_sems, out_sems
):
    tokens = inputs_hbm.shape[0]
    copies = [
        pltpu.make_async_copy(inputs_hbm, inputs.at[:tokens], in_sems.at[0]),
        pltpu.make_async_copy(theirs_hbm, inputs.at[tokens:], in_sems.at[1]),
        pltpu.make_async_copy(up_hbm, ups.at[:tokens], in_sems.at[2]),
        pltpu.make_async_copy(their_up_hbm, ups.at[tokens:], in_sems.at[3]),
    ]
    for copy in copies:
        copy.start()
    for copy in copies:
        copy.wait()
    stores = []
    for chunk in range(SIDE):
        total = lax.dot_general(
            core_columns(inputs, place_ref[1], chunk),
            ups[...],
            (((0,), (0,)), ((), ())),
            preferred_element_type=f32,
        )
        out[chunk] = (total * SCALE).astype(bf16)
        stores.append(pltpu.make_async_copy(out.at[chunk], out_hbm.at[chunk], out_sems.at[chunk]))
        stores[-1].start()
    for store in stores:
        store.wait()


def grad(place, inputs, theirs, up, their_up):
    tokens, width = inputs.shape
    features = up.shape[1]
    anywhere = pl.BlockSpec(memory_space=pl.ANY)
    return pl.pallas_call(
        grad_kernel,
        out_shape=jax.ShapeDtypeStruct((SIDE, ROWS, features), bf16),
        in_specs=[pl.BlockSpec(memory_space=pltpu.SMEM)] + [anywhere] * 4,
        out_specs=anywhere,
        scratch_shapes=[
            pltpu.VMEM((2 * tokens, width), bf16),
            pltpu.VMEM((2 * tokens, features), bf16),
            pltpu.VMEM((SIDE, ROWS, features), bf16),
            pltpu.SemaphoreType.DMA((4,)),
            pltpu.SemaphoreType.DMA((SIDE,)),
        ],
        cost_estimate=pl.CostEstimate(flops=1 << 30, bytes_accessed=6 << 20, transcendentals=0),
        compiler_params=pltpu.CompilerParams(vmem_limit_bytes=GRAD_VMEM_LIMIT),
        name="gradient",
    )(place, inputs, theirs, up, their_up)


def cast_kernel(after_ref, layer_ref, out_ref):
    out_ref[...] = layer_ref[0].astype(bf16)


def cast(layers, after):
    features = layers.shape[2]
    return pl.pallas_call(
        cast_kernel,
        out_shape=jax.ShapeDtypeStruct((PIECE, features), bf16),
        grid=(1,),
        in_specs=[
            pl.BlockSpec(memory_space=pl.ANY),
            pl.BlockSpec((1, PIECE, features), lambda i: (0, 0, 0)),
        ],
        out_specs=pl.BlockSpec((PIECE, features), lambda i: (0, 0)),
        cost_estimate=pl.CostEstimate(flops=0, bytes_accessed=1 << 20, transcendentals=0),
        name="cast_weights",
    )(after, layers)


def keys_kernel(
    place_ref, inputs_hbm, theirs_hbm, w0_hbm, w1_hbm, w2_hbm, w3_hbm, own_ref, other_ref, inputs, theirs, weights, sems
):
    sources = (w0_hbm, w1_hbm, w2_hbm, w3_hbm)
    offsets = (0, 1, 3, 2)
    loads = [
        pltpu.make_async_copy(inputs_hbm, inputs, sems.at[SIDE]),
        pltpu.make_async_copy(theirs_hbm, theirs, sems.at[SIDE + 1]),
    ]
    rows = [
        pltpu.make_async_copy(sources[offset], weights.at[offset], sems.at[offset])
        for offset in range(SIDE)
    ]
    rows[0].start()
    for load in loads:
        load.start()
    for offset in offsets[1:]:
        rows[offset].start()
    for load in loads:
        load.wait()
    own = 0.0
    other = 0.0
    for offset in offsets:
        chunk = lax.rem(place_ref[0] + SIDE - offset, SIDE)
        rows[offset].wait()
        own += jnp.dot(
            core_columns(inputs, place_ref[1], chunk), weights[offset], preferred_element_type=f32
        )
        other += jnp.dot(
            core_columns(theirs, place_ref[1], chunk), weights[offset], preferred_element_type=f32
        )
    own_ref[...] = own * SCALE
    other_ref[...] = (other * SCALE).astype(bf16)


def half_keys(place, inputs, theirs, weights):
    tokens, width = inputs.shape
    rows, features = weights[0].shape
    anywhere = pl.BlockSpec(memory_space=pl.ANY)
    whole = pl.BlockSpec(memory_space=pltpu.VMEM)
    return pl.pallas_call(
        keys_kernel,
        out_shape=(
            jax.ShapeDtypeStruct((tokens, features), f32),
            jax.ShapeDtypeStruct((tokens, features), bf16),
        ),
        in_specs=[pl.BlockSpec(memory_space=pltpu.SMEM)] + [anywhere] * (2 + SIDE),
        out_specs=(whole, whole),
        scratch_shapes=[
            pltpu.VMEM((tokens, width), bf16),
            pltpu.VMEM((tokens, width), bf16),
            pltpu.VMEM((SIDE, rows, features), bf16),
            pltpu.SemaphoreType.DMA((SIDE + 2,)),
        ],
        cost_estimate=pl.CostEstimate(flops=1 << 30, bytes_accessed=7 << 20, transcendentals=0),
        compiler_params=pltpu.CompilerParams(vmem_limit_bytes=KEYS_VMEM_LIMIT),
        name="half_keys",
    )(place, inputs, theirs, *weights)


def update_kernel(layers_ref, own_ref, other_ref, *refs):
    out_ref, keys_ref = refs[-2:]
    terms = [ref[...].astype(f32) for ref in refs[:-2]]
    while len(terms) > 1:
        terms = [first + second for first, second in zip(terms[::2], terms[1::2])]
    out_ref[0, 0] = layers_ref[0, 0] - inner_rate * terms[0]
    for layer in range(1, layers_ref.shape[1]):
        out_ref[0, layer] = layers_ref[0, layer]
    keys_ref[0] = (own_ref[...] + other_ref[...].astype(f32)).astype(bf16)


def update(pieces, local_weight, own, other):
    count, rows, features = local_weight.shape[1:]
    tokens = own.shape[0]
    steps = 2
    block = rows // steps
    layers = pl.BlockSpec((1, count, block, features), lambda i: (0, 0, i, 0))
    half = pl.BlockSpec((tokens // steps, features), lambda i: (i, 0))
    return pl.pallas_call(
        update_kernel,
        out_shape=(
            jax.ShapeDtypeStruct(local_weight.shape, f32),
            jax.ShapeDtypeStruct((1, tokens, features), bf16),
        ),
        grid=(steps,),
        in_specs=[layers, half, half]
        + [pl.BlockSpec((block, features), lambda i: (i, 0))] * len(pieces),
        out_specs=(layers, pl.BlockSpec((1, tokens // steps, features), lambda i: (0, i, 0))),
        cost_estimate=pl.CostEstimate(flops=1 << 19, bytes_accessed=3 << 20, transcendentals=0),
        compiler_params=pltpu.CompilerParams(vmem_limit_bytes=GRAD_VMEM_LIMIT),
        name="update",
    )(local_weight, own, other, *pieces)


def settle_kernel(
    chosen_ref,
    average_hbm,
    layers_hbm,
    outer_hbm,
    moment_hbm,
    layers_out,
    outer_out,
    moment_out,
    average,
    olds,
    news,
    in_sems,
    out_sems,
):
    chosen = chosen_ref[0]
    loads = [
        pltpu.make_async_copy(moment_hbm.at[chosen], olds.at[0], in_sems.at[0]),
        pltpu.make_async_copy(average_hbm, average, in_sems.at[1]),
        pltpu.make_async_copy(outer_hbm.at[chosen], olds.at[1], in_sems.at[2]),
        pltpu.make_async_copy(layers_hbm.at[0, chosen], olds.at[2], in_sems.at[3]),
    ]
    stores = [
        pltpu.make_async_copy(news.at[0], moment_out, out_sems.at[0]),
        pltpu.make_async_copy(news.at[1], outer_out, out_sems.at[1]),
        pltpu.make_async_copy(news.at[2], layers_out.at[0, chosen], out_sems.at[2]),
    ]
    for load in loads:
        load.start()
    loads[0].wait()
    loads[1].wait()
    news[0] = momentum_factor * olds[0] + average[...].astype(f32)
    stores[0].start()
    loads[2].wait()
    news[1] = olds[1] - outer_rate * (average[...].astype(f32) + momentum_factor * news[0])
    stores[1].start()
    loads[3].wait()
    news[2] = mixing * olds[2] + (1.0 - mixing) * news[1]
    stores[2].start()
    for store in stores:
        store.wait()


def settle(chosen, average, updated, outer_weight, outer_moment):
    rows, features = updated.shape[2:]
    anywhere = pl.BlockSpec(memory_space=pl.ANY)
    return pl.pallas_call(
        settle_kernel,
        out_shape=(
            jax.ShapeDtypeStruct(updated.shape, f32),
            jax.ShapeDtypeStruct((rows, features), f32),
            jax.ShapeDtypeStruct((rows, features), f32),
        ),
        in_specs=[pl.BlockSpec(memory_space=pltpu.SMEM)] + [anywhere] * 4,
        out_specs=(anywhere,) * 3,
        scratch_shapes=[
            pltpu.VMEM((rows, features), average.dtype),
            pltpu.VMEM((3, rows, features), f32),
            pltpu.VMEM((3, rows, features), f32),
            pltpu.SemaphoreType.DMA((4,)),
            pltpu.SemaphoreType.DMA((3,)),
        ],
        input_output_aliases={2: 0},
        cost_estimate=pl.CostEstimate(flops=1 << 20, bytes_accessed=2 << 20, transcendentals=0),
        compiler_params=pltpu.CompilerParams(vmem_limit_bytes=VMEM_LIMIT),
        name="settle",
    )(chosen, average, updated, outer_weight, outer_moment)


def sum_all(parts):
    terms = [parts[index].astype(f32) for index in range(parts.shape[0])]
    while len(terms) > 1:
        terms = [first + second for first, second in zip(terms[::2], terms[1::2])]
    return terms[0]


def spread(rows):
    return jnp.broadcast_to(rows.astype(bf16)[None], (SIDE,) + rows.shape)


def shift(offset):
    return [(source, (source + offset) % SIDE) for source in range(SIDE)]


swap = [(0, 1), (1, 0)]


def trained_step(activations, cotangent, local_weight, outer_weight, outer_moment, fragment_index):
    inputs = activations[0]
    upstream = cotangent[0]
    layers = local_weight[0]
    features = upstream.shape[1]
    place = jnp.stack([lax.axis_index(name) for name in ("x", "c")]).astype(jnp.int32)

    theirs = lax.ppermute(inputs, "c", swap)
    their_up = lax.ppermute(upstream, "c", swap)
    part = grad(place, inputs, theirs, upstream, their_up)
    rows = lax.all_gather(cast(layers, part), "zl", axis=0, tiled=True)
    delta = outer_weight[0] - layers[0]
    part = lax.all_to_all(part, "x", 0, 0)
    part, rows, delta = lax.optimization_barrier((part, rows, delta))

    part = sum_all(part).astype(bf16).reshape(SIDE, PIECE, features)
    part = lax.all_to_all(part, "zl", 0, 0)
    weights = [rows] + [lax.ppermute(rows, "x", shift(offset)) for offset in (1, 2, 3)]

    gradient = sum_all(part)
    mean = delta + inner_rate * gradient
    mean = mean.astype(bf16).reshape(SIDE, QUARTER, features)
    mean = sum_all(lax.all_to_all(mean, "y", 0, 0)) * (1.0 / (SIDE * SIDE))
    mean, weights[1], weights[3] = lax.optimization_barrier((mean, weights[1], weights[3]))
    mean = sum_all(lax.all_to_all(spread(mean), "zh", 0, 0))
    mean, gradient = lax.optimization_barrier((mean, gradient))
    mean = lax.all_to_all(spread(mean), "y", 0, 0).reshape(PIECE, features)

    own, other = half_keys(place, inputs, theirs, weights)
    other = lax.ppermute(other, "c", swap)
    updated, keys = update([gradient], local_weight, own, other)
    local_new, outer_new, moment_new = settle(
        fragment_index, mean, updated, outer_weight, outer_moment
    )
    return keys, local_new, outer_new, moment_new


def flip(mask):
    return [(source, source ^ mask) for source in range(SIDE)]


def other_step(activations, cotangent, local_weight, outer_weight, outer_moment, fragment_index):
    inputs = activations[0]
    upstream = cotangent[0]
    layers = local_weight[0]
    features = upstream.shape[1]
    place = jnp.stack([lax.axis_index(name) for name in ("x", "c")]).astype(jnp.int32)

    theirs = lax.ppermute(inputs, "c", swap)
    their_up = lax.ppermute(upstream, "c", swap)
    part = grad(place, inputs, theirs, upstream, their_up)
    rows = lax.all_gather(cast(layers, part), "zl", axis=0, tiled=True)
    pick = lambda array: lax.dynamic_index_in_dim(array, fragment_index[0], 0, keepdims=False)
    delta = (pick(outer_weight) - pick(layers)).astype(bf16).reshape(SIDE, QUARTER, features)
    part = lax.all_to_all(part, "x", 0, 0)
    part, rows, delta = lax.optimization_barrier((part, rows, delta))
    weights = [rows] + [lax.ppermute(rows, "x", shift(offset)) for offset in (1, 2, 3)]

    mean = sum_all(lax.all_to_all(delta, "y", 0, 0)) * (1.0 / (SIDE * SIDE))
    part = sum_all(part).astype(bf16).reshape(SIDE, PIECE, features)
    mean = sum_all(lax.all_to_all(spread(mean), "zh", 0, 0))
    mean = lax.all_to_all(spread(mean), "y", 0, 0).reshape(PIECE, features)

    along = lax.axis_index("zl")
    chunk = lambda mask: lax.dynamic_index_in_dim(part, along ^ mask, 0, keepdims=False)
    pieces = [chunk(0)] + [lax.ppermute(chunk(mask), "zl", flip(mask)) for mask in (1, 2, 3)]

    own, other = half_keys(place, inputs, theirs, weights)
    other = lax.ppermute(other, "c", swap)
    updated, keys = update(pieces, local_weight, own, other)
    local_new, outer_new, moment_new = settle(
        fragment_index, mean, updated, outer_weight, outer_moment
    )
    return keys, local_new, outer_new, moment_new


def shards(activations, cotangent, local_weight, outer_weight, outer_moment, fragment_index):
    return lax.cond(
        fragment_index[0] == 0,
        trained_step,
        other_step,
        activations,
        cotangent,
        local_weight,
        outer_weight,
        outer_moment,
        fragment_index,
    )


def solution(mesh):
    fine = Mesh(
        mesh.devices.reshape(SIDE, SIDE, SIDE, SIDE, CORES), ("zh", "y", "x", "zl", "c")
    )
    replica = ("zh", "y")
    fsdp = ("x", "zl", "c")
    in_specs = (
        P(replica, fsdp, None),
        P(replica, fsdp, None),
        P(replica, None, fsdp, None),
        P(None, fsdp, None),
        P(None, fsdp, None),
        P(),
    )
    out_specs = (
        P(replica, fsdp, None),
        P(replica, None, fsdp, None),
        P(fsdp, None),
        P(fsdp, None),
    )
    return jax.shard_map(shards, mesh=fine, in_specs=in_specs, out_specs=out_specs, check_vma=False)
```
